256 devices in a mesh: node: 64 (over x, z_hi, y, core), local: 4 (over z_lo).
Axes of the slice: x: 4, y: 4, z: 8 (z_hi: 2, z_lo: 4; z = z_hi * 4 + z_lo), core: 2. Of those that a mesh axis runs over, the one named last changes fastest.
Arguments:
- tokens: bfloat16 [32768, 4096], P(('node', 'local')), may hold values from -24 to 24
- cotangent: bfloat16 [32768, 4096], P(('node', 'local')), may hold values from -0.03125 to 0.03125
- master: float32 [4096, 4096], P('node', 'local'), may hold values from -3 to 3
- moment: float32 [4096, 4096], P('node', 'local'), may hold values from -5 to 5
- second: float32 [4096, 4096], P('node', 'local'), may hold values from 0.1 to 2
Outputs:
- master_new: float32 [4096, 4096], P('node', 'local')
- moment_new: float32 [4096, 4096], P('node', 'local')
- second_new: float32 [4096, 4096], P('node', 'local')
- weights: bfloat16 [4096, 4096], P(None, 'local')
The draws below stay inside these ranges and needn't reach their ends.
All inputs are finite; a program needn't handle non-finite values.
Results may differ from the reference program's by a relative error of at most 0.001.
Values may be sent and summed in bfloat16 or wider, within the bound.
A program may use at most 192 MiB of HBM per device.

```python
import math
import jax
import jax.numpy as jnp
from jax import lax

D_IN = 4096
D_OUT = 4096
TOKENS = 32768


def with_spikes(values, own_key, source, target, parts, factor):
    owner, partner = [(jnp.arange(values.shape[position]) // (values.shape[position] // parts)).reshape([-1 if axis == position else 1 for axis in range(values.ndim)]) for position in (source, target)]
    chosen = jax.random.permutation(own_key, parts)[partner]
    strong = (owner == chosen) | (owner == (partner + parts // 2) % parts)
    return jnp.where(strong, factor * values, values)


def steps_of(key, shape, cuts, low, top_value):
    factor_of, own = 1.0, jax.random.fold_in(key, 6)
    for position, blocks in cuts:
        draws = jnp.exp(jax.random.uniform(jax.random.fold_in(own, position), (blocks,), jnp.float32, low / len(cuts), top_value / len(cuts)))
        factor_of = factor_of * jnp.repeat(draws, shape[position] // blocks).reshape([-1 if axis == position else 1 for axis in range(len(shape))])
    return factor_of


def noise(stream_key, dims, spread, limit, cuts=(), dtype=jnp.bfloat16):
    drawn = spread * jax.random.normal(stream_key, dims, jnp.float32)
    if cuts:
        drawn = drawn * steps_of(stream_key, dims, cuts, -0.22, 0.18)
    return jnp.clip(drawn, -limit, limit).astype(dtype)


def bell_draw_with(own_key, shape, deviation, limit, cuts, heavy, kind=jnp.bfloat16):
    entries = deviation * jax.random.normal(own_key, shape, jnp.float32)
    if cuts:
        entries = entries * steps_of(own_key, shape, cuts, -0.22, 0.18)
    return jnp.clip(with_spikes(entries, jax.random.fold_in(own_key, 3), *heavy), -limit, limit).astype(kind)


def setup_inputs(seed: int = 0) -> dict:
    key_list = jax.random.split(jax.random.key(seed), 6)
    tokens = bell_draw_with(key_list[0], (TOKENS, D_IN), 1.0, 24.0, ((0, 256),), (0, 1, 256, 6.0))
    cotangent = noise(key_list[1], (TOKENS, D_OUT), TOKENS ** -0.5, 0.03125, ((0, 256),))
    master = noise(key_list[2], (D_IN, D_OUT), 0.5, 3.0, ((0, 64), (1, 4)), jnp.float32)
    moment = noise(key_list[3], (D_IN, D_OUT), 1.0, 5.0, ((0, 64), (1, 4)), jnp.float32)
    second = jnp.clip(jnp.exp(math.log(2.0) - 2.9957323 * jax.random.uniform(key_list[4], (D_IN, D_OUT), jnp.float32) ** steps_of(key_list[4], (D_IN, D_OUT), ((0, 64), (1, 4)), -0.2, 0.2)), 0.1, 2.0)
    return {"tokens": tokens, "cotangent": cotangent, "master": master, "moment": moment, "second": second}


first_beta = 0.9
second_beta = 0.95
learn_rate = 0.01
decay_rate = 0.1
epsilon = 1e-08
first_fix = 1.0 - 0.9 ** 20
second_fix = 1.0 - 0.95 ** 20

def reference(tokens, cotangent, master, moment, second):
    gradient = lax.dot_general(tokens, cotangent, (((0,), (0,)), ((), ())), preferred_element_type=jnp.float32)
    moment_new = first_beta * moment + (1.0 - first_beta) * gradient
    second_new = second_beta * second + (1.0 - second_beta) * gradient * gradient
    update = moment_new / first_fix / (jnp.sqrt(second_new / second_fix) + epsilon) + decay_rate * master
    master_new = master - learn_rate * update
    weights = master_new.astype(jnp.bfloat16)
    return (master_new, moment_new, second_new, weights)
```

```python
import jax
import jax.numpy as jnp
from jax import lax
from jax.experimental import pallas as pl
from jax.experimental.pallas import tpu as pltpu
from jax.sharding import PartitionSpec as P

MESH = pl.DeviceIdType.MESH

first_beta = 0.9
second_beta = 0.95
learn_rate = 0.01
decay_rate = 0.1
epsilon = 1e-08
first_fix = 1.0 - 0.9**20
second_fix = 1.0 - 0.95**20

SLICES = 4
SR = 64 // SLICES


def kernel(
    tok, cot, master, moment, second,
    master_new, moment_new, second_new, weights,
    tg, cg, part, core_in, z_in, grad, shard, ssem, rsem, lsem,
):
    node, l = lax.axis_index("node"), lax.axis_index("local")
    c = node % 2
    y = (node // 2) % 4
    h = (node // 8) % 2
    x = node // 16
    z = h * 4 + l

    def dev(dx=0, dy=0, dz=0, dc=0):
        zz = (z + dz + 8) % 8
        xx, yy, cc = (x + dx + 4) % 4, (y + dy + 4) % 4, (c + dc) % 2
        return (((xx * 2 + zz // 4) * 4 + yy) * 2 + cc, zz % 4)

    count = [0]

    def ids(n=1):
        first = count[0]
        count[0] += n
        return first

    def rcopy(src, dst, sid, to):
        return pltpu.make_async_remote_copy(
            src_ref=src, dst_ref=dst, send_sem=ssem.at[sid], recv_sem=rsem.at[sid],
            device_id=to, device_id_type=MESH,
        )

    sent = []

    def start(cp):
        cp.start()
        sent.append(cp)

    barrier = pltpu.get_barrier_semaphore()
    peers = [dev(dx=d) for d in (1, 2, 3)] + [dev(dy=d) for d in (1, 2, 3)]
    peers += [dev(dz=1), dev(dz=-1), dev(dz=4), dev(dc=1)]
    for p in peers:
        pl.semaphore_signal(barrier, inc=1, device_id=p, device_id_type=MESH)
    pl.semaphore_wait(barrier, len(peers))

    def cols(b):
        return pl.ds(pl.multiple_of(b * 1024, 1024), 1024)

    def slot(buf, ry, rx, lo=0, n=128):
        return buf.at[ry, pl.ds(rx * 128 + lo, n)]

    own_t, own_c = tok.at[:, cols(x)], cot.at[:, cols(y)]
    lt = pltpu.make_async_copy(own_t, slot(tg, 0, 0), lsem.at[0])
    lc = pltpu.make_async_copy(own_c, slot(cg, 0, 0), lsem.at[1])
    lt.start()
    lc.start()
    ta, ca = {}, {}
    for d in (1, 3, 2):
        r = (4 - d) % 4
        ta[r] = rcopy(tok.at[:, cols((x + d) % 4)], slot(tg, 0, r), ids(), dev(dx=d))
        ca[r] = rcopy(cot.at[:, cols((y + d) % 4)], slot(cg, r, 0), ids(), dev(dy=d))
        start(ta[r])
        start(ca[r])
    tp, tm, cp_, cm = {}, {}, {}, {}

    def spread_t(rx):
        src = own_t if rx == 0 else slot(tg, 0, rx)
        tp[rx] = rcopy(src, slot(tg, 3, rx), ids(), dev(dy=1))
        tm[rx] = rcopy(src, slot(tg, 1, rx), ids(), dev(dy=-1))
        start(tp[rx])
        start(tm[rx])

    def spread_c(ry):
        src = own_c if ry == 0 else slot(cg, ry, 0)
        cp_[ry] = rcopy(src, slot(cg, ry, 3), ids(), dev(dx=1))
        cm[ry] = rcopy(src, slot(cg, ry, 1), ids(), dev(dx=-1))
        start(cp_[ry])
        start(cm[ry])

    spread_t(0)
    spread_c(0)
    for r in (3, 1, 2):
        ta[r].wait_recv()
        spread_t(r)
        ca[r].wait_recv()
        spread_c(r)
    tfp, tfm, cfp, cfm = {}, {}, {}, {}
    lt.wait()
    lc.wait()

    def forward(r):
        tp[r].wait_recv()
        tfp[r] = rcopy(slot(tg, 3, r, 0, 64), slot(tg, 2, r, 0, 64), ids(), dev(dy=1))
        start(tfp[r])
        cp_[r].wait_recv()
        cfp[r] = rcopy(slot(cg, r, 3, 0, 64), slot(cg, r, 2, 0, 64), ids(), dev(dx=1))
        start(cfp[r])
        tm[r].wait_recv()
        tfm[r] = rcopy(slot(tg, 1, r, 64, 64), slot(tg, 2, r, 64, 64), ids(), dev(dy=-1))
        start(tfm[r])
        cm[r].wait_recv()
        cfm[r] = rcopy(slot(cg, r, 1, 64, 64), slot(cg, r, 2, 64, 64), ids(), dev(dx=-1))
        start(cfm[r])

    def tile(ry, m, first):
        rows = pl.ds(pl.multiple_of(m * 256, 256), 256)
        for n in range(2):
            out = pl.ds(n * 512, 512)
            got = lax.dot_general(
                tg[ry, :, rows], cg[ry, :, out], (((0,), (0,)), ((), ())),
                preferred_element_type=jnp.float32,
            )
            part[rows, out] = got if first else part[rows, out] + got

    def matmul(ry, first):
        @pl.loop(0, 4)
        def _(m):
            tile(ry, m, first)

    forward(0)
    forward(3)
    cfp[0].wait_recv()
    cfm[0].wait_recv()
    matmul(0, True)
    forward(1)
    cfp[3].wait_recv()
    cfm[3].wait_recv()
    forward(2)
    matmul(3, False)
    cfp[1].wait_recv()
    cfm[1].wait_recv()
    matmul(1, False)
    cfp[2].wait_recv()
    cfm[2].wait_recv()
    for r in range(4):
        tfp[r].wait_recv()
        tfm[r].wait_recv()

    core_id = ids(8)

    def block(hh, yy, cc, lo=0, n=64):
        return pl.ds(pl.multiple_of(hh * 512 + yy * 128 + cc * 64 + lo, n), n)

    def core_copy(hh, yy):
        return rcopy(
            part.at[block(hh, yy, 1 - c)], core_in.at[hh, yy], core_id + hh * 4 + yy, dev(dc=1)
        )

    for m in range(4):
        tile(2, m, False)
        for b in (2 * m, 2 * m + 1):
            start(core_copy(b // 4, b % 4))

    r = (z - y + 8) % 8
    q = r % 4
    end = q == 0
    z_id = [ids(4 * SLICES), ids(4 * SLICES)]
    g_id = ids(4 * SLICES)

    def z_copy(way, hh, s, yy):
        return rcopy(
            part.at[block(hh, yy, c, s * SR, SR)], z_in.at[way, s, yy],
            z_id[way] + s * 4 + yy, dev(dz=1 - 2 * way),
        )

    def g_copy(s, yy):
        return pltpu.make_async_remote_copy(
            src_ref=part.at[block(h, yy, c, s * SR, SR)], dst_ref=grad.at[s],
            send_sem=ssem.at[g_id + s * 4 + yy], recv_sem=rsem.at[g_id + s],
            device_id=(((x * 2 + h) * 4 + yy) * 2 + c, l), device_id_type=MESH,
        )

    def core_sum(hh, yy):
        core_copy(hh, yy).wait_recv()
        part[block(hh, yy, c)] += core_in[hh, yy]

    order = ((2, 3, 0, 1), (0, 1, 2, 3))

    @pl.when(jnp.logical_not(end))
    def _():
        up = jnp.where(r < 4, 1, 0)
        for s in range(SLICES):
            for i in range(4):
                for way in range(2):
                    hh = up if way == 0 else 1 - up
                    yy = order[way][i]
                    if s == 0:
                        core_sum(hh, yy)

                    def add():
                        z_copy(way, hh, s, yy).wait_recv()
                        rows = block(hh, yy, c, s * SR, SR)
                        part[rows] += z_in[way, s, yy]

                    if i < 2:
                        pl.when(q != (1 if way == 0 else 3))(add)
                    else:
                        add()
                    z_copy(way, hh, s, yy).start()

    @pl.when(end)
    def _():
        for i in range(2):
            for way in range(2):
                core_sum(1 - h, order[way][i + 2])
        for s in range(SLICES):
            for i in range(2):
                for way in range(2):
                    z_copy(way, 1 - h, s, order[way][i + 2]).start()
        for yy in range(4):
            core_sum(h, yy)
        for s in range(SLICES):
            for yy in range(4):
                z_copy(0, h, s, yy).wait_recv()
                z_copy(1, h, s, yy).wait_recv()
                rows = block(h, yy, c, s * SR, SR)
                total = part[rows] + (z_in[0, s, yy] + z_in[1, s, yy])
                part[rows] = total

                @pl.when(yy == y)
                def _():
                    grad[s] = total

                @pl.when(yy != y)
                def _():
                    g_copy(s, yy).start()

    for s in range(SLICES):
        @pl.when(jnp.logical_not(end))
        def _():
            g_copy(s, 0).wait_recv()

        rows = pl.ds(s * SR, SR)
        g = grad[s]
        m_new = first_beta * moment[rows] + (1.0 - first_beta) * g
        s_new = second_beta * second[rows] + (1.0 - second_beta) * g * g
        old = master[rows]
        update = m_new / first_fix / (jnp.sqrt(s_new / second_fix) + epsilon) + decay_rate * old
        new = old - learn_rate * update
        master_new[rows] = new
        moment_new[rows] = m_new
        second_new[rows] = s_new
        shard[rows] = new.astype(jnp.bfloat16)

    def da(d):
        return dev(dx=d * (1 - c), dy=d * c)

    def db(d):
        return dev(dx=d * c, dy=d * (1 - c))

    def unit(hh, a=0, b=0):
        xx = (x + a * (1 - c) + b * c + 4) % 4
        yy = (y + a * c + b * (1 - c) + 4) % 4
        return weights.at[xx, hh, yy, c]

    both = slice(None)
    side = dev(dc=1)
    own = pltpu.make_async_copy(shard, unit(h), lsem.at[2])
    own.start()
    w_z = rcopy(shard, unit(h), ids(), dev(dz=4))
    w_a = {(0, 1): rcopy(shard, unit(h), ids(), da(1)), (0, -1): rcopy(shard, unit(h), ids(), da(-1))}
    start(w_z)
    start(w_a[0, 1])
    start(w_a[0, -1])
    sib = []

    def to_side(hh, a=0, b=0):
        cp = rcopy(unit(hh, a, b), unit(hh, a, b), ids(), side)
        start(cp)
        sib.append(cp)

    own.wait()
    to_side(h)
    w_z.wait_recv()
    for d in (1, -1):
        w_a[1, d] = rcopy(unit(1 - h), unit(1 - h), ids(), da(d))
        start(w_a[1, d])
    to_side(1 - h)
    w_b = {}

    def b_send(a):
        for d in (1, -1):
            w_b[a, d] = rcopy(unit(both, a), unit(both, a), ids(), db(d))
            start(w_b[a, d])

    b_send(0)
    f_a = {}
    w_a[0, 1].wait_recv()
    f_a[1] = rcopy(unit(h, -1), unit(h, -1), ids(), da(1))
    start(f_a[1])
    w_a[1, -1].wait_recv()
    f_a[-1] = rcopy(unit(1 - h, 1), unit(1 - h, 1), ids(), da(-1))
    start(f_a[-1])
    w_a[1, 1].wait_recv()
    b_send(-1)
    w_a[0, -1].wait_recv()
    b_send(1)
    to_side(both, -1)
    to_side(both, 1)
    f_a[1].wait_recv()
    f_a[-1].wait_recv()
    b_send(2)
    to_side(both, 2)
    f_b = {}
    for a in (0, -1, 1, 2):
        w_b[a, 1].wait_recv()
        f_b[a, 1] = rcopy(unit(0, a, -1), unit(0, a, -1), ids(), db(1))
        start(f_b[a, 1])
        w_b[a, -1].wait_recv()
        f_b[a, -1] = rcopy(unit(1, a, 1), unit(1, a, 1), ids(), db(-1))
        start(f_b[a, -1])
        to_side(both, a, -1)
        to_side(both, a, 1)
    for a in (0, -1, 1, 2):
        f_b[a, 1].wait_recv()
        f_b[a, -1].wait_recv()
        to_side(both, a, 2)
    for cp in sib:
        cp.wait_recv()
    for cp in sent:
        cp.wait_send()

    @pl.when(jnp.logical_not(end))
    def _():
        for s in range(SLICES):
            for yy in range(4):
                for way in range(2):
                    z_copy(way, 0, s, yy).wait_send()

    @pl.when(end)
    def _():
        for s in range(SLICES):
            for i in range(2):
                for way in range(2):
                    z_copy(way, 1 - h, s, order[way][i + 2]).wait_send()
            for yy in range(4):
                @pl.when(yy != y)
                def _():
                    g_copy(s, yy).wait_send()


N_SEM = 256


def on_device(tokens, cotangent, master, moment, second):
    vmem, hbm = pl.BlockSpec(memory_space=pltpu.VMEM), pl.BlockSpec(memory_space=pl.ANY)
    f32 = jax.ShapeDtypeStruct((64, 1024), jnp.float32)
    out = pl.pallas_call(
        kernel,
        out_shape=(f32, f32, f32, jax.ShapeDtypeStruct((4, 2, 4, 2, 64, 1024), jnp.bfloat16)),
        in_specs=[hbm, hbm, vmem, vmem, vmem],
        out_specs=(vmem, vmem, vmem, hbm),
        scratch_shapes=[
            pltpu.VMEM((4, 512, 1024), jnp.bfloat16),
            pltpu.VMEM((4, 512, 1024), jnp.bfloat16),
            pltpu.VMEM((1024, 1024), jnp.float32),
            pltpu.VMEM((2, 4, 64, 1024), jnp.float32),
            pltpu.VMEM((2, SLICES, 4, SR, 1024), jnp.float32),
            pltpu.VMEM((SLICES, SR, 1024), jnp.float32),
            pltpu.VMEM((64, 1024), jnp.bfloat16),
            pltpu.SemaphoreType.DMA((N_SEM,)),
            pltpu.SemaphoreType.DMA((N_SEM,)),
            pltpu.SemaphoreType.DMA((3,)),
        ],
        compiler_params=pltpu.CompilerParams(
            collective_id=0, has_side_effects=True, vmem_limit_bytes=48 * 2**20
        ),
    )(tokens, cotangent, master, moment, second)
    return (*out[:3], out[3].reshape(4096, 1024))


def solution(mesh):
    placed = (
        P(("node", "local"), None),
        P(("node", "local"), None),
        P("node", "local"),
        P("node", "local"),
        P("node", "local"),
    )
    return jax.shard_map(
        on_device,
        mesh=mesh,
        in_specs=placed,
        out_specs=(P("node", "local"), P("node", "local"), P("node", "local"), P(None, "local")),
        check_vma=False,
    )
```

```python
import jax
import jax.numpy as jnp
from jax import lax
from jax.experimental import pallas as pl
from jax.experimental.pallas import tpu as pltpu
from jax.sharding import PartitionSpec as P

MESH = pl.DeviceIdType.MESH

first_beta = 0.9
second_beta = 0.95
learn_rate = 0.01
decay_rate = 0.1
epsilon = 1e-08
first_fix = 1.0 - 0.9**20
second_fix = 1.0 - 0.95**20

LAG = 2
SLICES = 4
SR = 64 // SLICES


def kernel(
    tok, cot, master, moment, second,
    master_new, moment_new, second_new, weights,
    tg, cg, part, core_in, z_in, grad, shard, ssem, rsem, lsem,
):
    node, l = lax.axis_index("node"), lax.axis_index("local")
    c = node % 2
    y = (node // 2) % 4
    h = (node // 8) % 2
    x = node // 16
    z = h * 4 + l

    def dev(dx=0, dy=0, dz=0, dc=0):
        zz = (z + dz + 8) % 8
        xx, yy, cc = (x + dx + 4) % 4, (y + dy + 4) % 4, (c + dc) % 2
        return (((xx * 2 + zz // 4) * 4 + yy) * 2 + cc, zz % 4)

    count = [0]

    def ids(n=1):
        first = count[0]
        count[0] += n
        return first

    def rcopy(src, dst, sid, to):
        return pltpu.make_async_remote_copy(
            src_ref=src, dst_ref=dst, send_sem=ssem.at[sid], recv_sem=rsem.at[sid],
            device_id=to, device_id_type=MESH,
        )

    sent = []

    def start(cp):
        cp.start()
        sent.append(cp)

    barrier = pltpu.get_barrier_semaphore()
    peers = [dev(dx=d) for d in (1, 2, 3)] + [dev(dy=d) for d in (1, 2, 3)]
    peers += [dev(dz=1), dev(dz=-1), dev(dz=4), dev(dc=1)]
    for p in peers:
        pl.semaphore_signal(barrier, inc=1, device_id=p, device_id_type=MESH)
    pl.semaphore_wait(barrier, len(peers))

    def cols(b):
        return pl.ds(pl.multiple_of(b * 1024, 1024), 1024)

    def slot(buf, ry, rx, lo=0, n=128):
        return buf.at[ry, pl.ds(rx * 128 + lo, n)]

    own_t, own_c = tok.at[:, cols(x)], cot.at[:, cols(y)]
    lt = pltpu.make_async_copy(own_t, slot(tg, 0, 0), lsem.at[0])
    lc = pltpu.make_async_copy(own_c, slot(cg, 0, 0), lsem.at[1])
    lt.start()
    lc.start()
    ta, ca = {}, {}
    for d in (1, 3, 2):
        r = (4 - d) % 4
        ta[r] = rcopy(tok.at[:, cols((x + d) % 4)], slot(tg, 0, r), ids(), dev(dx=d))
        ca[r] = rcopy(cot.at[:, cols((y + d) % 4)], slot(cg, r, 0), ids(), dev(dy=d))
        start(ta[r])
        start(ca[r])
    tp, tm, cp_, cm = {}, {}, {}, {}

    def spread_t(rx):
        src = own_t if rx == 0 else slot(tg, 0, rx)
        tp[rx] = rcopy(src, slot(tg, 3, rx), ids(), dev(dy=1))
        tm[rx] = rcopy(src, slot(tg, 1, rx), ids(), dev(dy=-1))
        start(tp[rx])
        start(tm[rx])

    def spread_c(ry):
        src = own_c if ry == 0 else slot(cg, ry, 0)
        cp_[ry] = rcopy(src, slot(cg, ry, 3), ids(), dev(dx=1))
        cm[ry] = rcopy(src, slot(cg, ry, 1), ids(), dev(dx=-1))
        start(cp_[ry])
        start(cm[ry])

    spread_t(0)
    spread_c(0)
    for r in (3, 1, 2):
        ta[r].wait_recv()
        spread_t(r)
        ca[r].wait_recv()
        spread_c(r)
    tfp, tfm, cfp, cfm = {}, {}, {}, {}
    lt.wait()
    lc.wait()

    def forward(r):
        tp[r].wait_recv()
        tfp[r] = rcopy(slot(tg, 3, r, 0, 64), slot(tg, 2, r, 0, 64), ids(), dev(dy=1))
        start(tfp[r])
        cp_[r].wait_recv()
        cfp[r] = rcopy(slot(cg, r, 3, 0, 64), slot(cg, r, 2, 0, 64), ids(), dev(dx=1))
        start(cfp[r])
        tm[r].wait_recv()
        tfm[r] = rcopy(slot(tg, 1, r, 64, 64), slot(tg, 2, r, 64, 64), ids(), dev(dy=-1))
        start(tfm[r])
        cm[r].wait_recv()
        cfm[r] = rcopy(slot(cg, r, 1, 64, 64), slot(cg, r, 2, 64, 64), ids(), dev(dx=-1))
        start(cfm[r])

    def tile(ry, m, first):
        rows = pl.ds(pl.multiple_of(m * 256, 256), 256)
        for n in range(2):
            out = pl.ds(n * 512, 512)
            got = lax.dot_general(
                tg[ry, :, rows], cg[ry, :, out], (((0,), (0,)), ((), ())),
                preferred_element_type=jnp.float32,
            )
            part[rows, out] = got if first else part[rows, out] + got

    def matmul(ry, first):
        @pl.loop(0, 4)
        def _(m):
            tile(ry, m, first)

    forward(0)
    forward(3)
    cfp[0].wait_recv()
    cfm[0].wait_recv()
    matmul(0, True)
    forward(1)
    cfp[3].wait_recv()
    cfm[3].wait_recv()
    forward(2)
    matmul(3, False)
    cfp[1].wait_recv()
    cfm[1].wait_recv()
    matmul(1, False)
    cfp[2].wait_recv()
    cfm[2].wait_recv()
    for r in range(4):
        tfp[r].wait_recv()
        tfm[r].wait_recv()

    core_id = ids(8)

    def block(hh, yy, cc, lo=0, n=64):
        return pl.ds(pl.multiple_of(hh * 512 + yy * 128 + cc * 64 + lo, n), n)

    def core_copy(hh, yy):
        return rcopy(
            part.at[block(hh, yy, 1 - c)], core_in.at[hh, yy], core_id + hh * 4 + yy, dev(dc=1)
        )

    for m in range(4):
        tile(2, m, False)
        for b in (2 * m, 2 * m + 1):
            start(core_copy(b // 4, b % 4))

    r = (z - y + 8) % 8
    q = r % 4
    end = q == 0
    z_id = [ids(4 * SLICES), ids(4 * SLICES)]
    g_id = ids(4 * SLICES)

    def z_copy(way, hh, s, yy):
        return rcopy(
            part.at[block(hh, yy, c, s * SR, SR)], z_in.at[way, s, yy],
            z_id[way] + s * 4 + yy, dev(dz=1 - 2 * way),
        )

    def g_copy(s, yy):
        return pltpu.make_async_remote_copy(
            src_ref=part.at[block(h, yy, c, s * SR, SR)], dst_ref=grad.at[s],
            send_sem=ssem.at[g_id + s * 4 + yy], recv_sem=rsem.at[g_id + s],
            device_id=(((x * 2 + h) * 4 + yy) * 2 + c, l), device_id_type=MESH,
        )

    def core_sum(hh, yy):
        core_copy(hh, yy).wait_recv()
        part[block(hh, yy, c)] += core_in[hh, yy]

    order = ((2, 3, 0, 1), (0, 1, 2, 3))

    up = jnp.where(r < 4, 1, 0)
    for place in (1, 2, 3):
        steps = [(k + LAG * (place - 1 if way == 0 else 3 - place), way, k) for k in range(4 * SLICES) for way in range(2)]

        @pl.when(q == place)
        def _():
            for _, way, k in sorted(steps):
                hh = up if way == 0 else 1 - up
                s, i = k // 4, k % 4
                yy = order[way][i]
                if s == 0:
                    core_sum(hh, yy)
                if i >= 2 or place != (1 if way == 0 else 3):
                    z_copy(way, hh, s, yy).wait_recv()
                    rows = block(hh, yy, c, s * SR, SR)
                    part[rows] += z_in[way, s, yy]
                z_copy(way, hh, s, yy).start()

    @pl.when(end)
    def _():
        for i in range(2):
            for way in range(2):
                core_sum(1 - h, order[way][i + 2])
        for s in range(SLICES):
            for i in range(2):
                for way in range(2):
                    z_copy(way, 1 - h, s, order[way][i + 2]).start()
        for yy in range(4):
            core_sum(h, yy)
        for s in range(SLICES):
            for yy in range(4):
                z_copy(0, h, s, yy).wait_recv()
                z_copy(1, h, s, yy).wait_recv()
                rows = block(h, yy, c, s * SR, SR)
                total = part[rows] + (z_in[0, s, yy] + z_in[1, s, yy])
                part[rows] = total

                @pl.when(yy == y)
                def _():
                    grad[s] = total

                @pl.when(yy != y)
                def _():
                    g_copy(s, yy).start()

    for s in range(SLICES):
        @pl.when(jnp.logical_not(end))
        def _():
            g_copy(s, 0).wait_recv()

        rows = pl.ds(s * SR, SR)
        g = grad[s]
        m_new = first_beta * moment[rows] + (1.0 - first_beta) * g
        s_new = second_beta * second[rows] + (1.0 - second_beta) * g * g
        old = master[rows]
        update = m_new / first_fix / (jnp.sqrt(s_new / second_fix) + epsilon) + decay_rate * old
        new = old - learn_rate * update
        master_new[rows] = new
        moment_new[rows] = m_new
        second_new[rows] = s_new
        shard[rows] = new.astype(jnp.bfloat16)

    def da(d):
        return dev(dx=d * (1 - c), dy=d * c)

    def db(d):
        return dev(dx=d * c, dy=d * (1 - c))

    def unit(hh, a=0, b=0):
        xx = (x + a * (1 - c) + b * c + 4) % 4
        yy = (y + a * c + b * (1 - c) + 4) % 4
        return weights.at[xx, hh, yy, c]

    both = slice(None)
    side = dev(dc=1)
    own = pltpu.make_async_copy(shard, unit(h), lsem.at[2])
    own.start()
    w_z = rcopy(shard, unit(h), ids(), dev(dz=4))
    w_a = {(0, 1): rcopy(shard, unit(h), ids(), da(1)), (0, -1): rcopy(shard, unit(h), ids(), da(-1))}
    start(w_z)
    start(w_a[0, 1])
    start(w_a[0, -1])
    sib = []

    def to_side(hh, a=0, b=0):
        cp = rcopy(unit(hh, a, b), unit(hh, a, b), ids(), side)
        start(cp)
        sib.append(cp)

    own.wait()
    to_side(h)
    w_z.wait_recv()
    for d in (1, -1):
        w_a[1, d] = rcopy(unit(1 - h), unit(1 - h), ids(), da(d))
        start(w_a[1, d])
    to_side(1 - h)
    w_b = {}

    def b_send(a):
        for d in (1, -1):
            w_b[a, d] = rcopy(unit(both, a), unit(both, a), ids(), db(d))
            start(w_b[a, d])

    b_send(0)
    f_a = {}
    w_a[0, 1].wait_recv()
    f_a[1] = rcopy(unit(h, -1), unit(h, -1), ids(), da(1))
    start(f_a[1])
    w_a[1, -1].wait_recv()
    f_a[-1] = rcopy(unit(1 - h, 1), unit(1 - h, 1), ids(), da(-1))
    start(f_a[-1])
    w_a[1, 1].wait_recv()
    b_send(-1)
    w_a[0, -1].wait_recv()
    b_send(1)
    to_side(both, -1)
    to_side(both, 1)
    f_a[1].wait_recv()
    f_a[-1].wait_recv()
    b_send(2)
    to_side(both, 2)
    f_b = {}
    for a in (0, -1, 1, 2):
        w_b[a, 1].wait_recv()
        f_b[a, 1] = rcopy(unit(0, a, -1), unit(0, a, -1), ids(), db(1))
        start(f_b[a, 1])
        w_b[a, -1].wait_recv()
        f_b[a, -1] = rcopy(unit(1, a, 1), unit(1, a, 1), ids(), db(-1))
        start(f_b[a, -1])
        to_side(both, a, -1)
        to_side(both, a, 1)
    for a in (0, -1, 1, 2):
        f_b[a, 1].wait_recv()
        f_b[a, -1].wait_recv()
        to_side(both, a, 2)
    for cp in sib:
        cp.wait_recv()
    for cp in sent:
        cp.wait_send()

    @pl.when(jnp.logical_not(end))
    def _():
        for s in range(SLICES):
            for yy in range(4):
                for way in range(2):
                    z_copy(way, 0, s, yy).wait_send()

    @pl.when(end)
    def _():
        for s in range(SLICES):
            for i in range(2):
                for way in range(2):
                    z_copy(way, 1 - h, s, order[way][i + 2]).wait_send()
            for yy in range(4):
                @pl.when(yy != y)
                def _():
                    g_copy(s, yy).wait_send()


N_SEM = 256


def on_device(tokens, cotangent, master, moment, second):
    vmem, hbm = pl.BlockSpec(memory_space=pltpu.VMEM), pl.BlockSpec(memory_space=pl.ANY)
    f32 = jax.ShapeDtypeStruct((64, 1024), jnp.float32)
    out = pl.pallas_call(
        kernel,
        out_shape=(f32, f32, f32, jax.ShapeDtypeStruct((4, 2, 4, 2, 64, 1024), jnp.bfloat16)),
        in_specs=[hbm, hbm, vmem, vmem, vmem],
        out_specs=(vmem, vmem, vmem, hbm),
        scratch_shapes=[
            pltpu.VMEM((4, 512, 1024), jnp.bfloat16),
            pltpu.VMEM((4, 512, 1024), jnp.bfloat16),
            pltpu.VMEM((1024, 1024), jnp.float32),
            pltpu.VMEM((2, 4, 64, 1024), jnp.float32),
            pltpu.VMEM((2, SLICES, 4, SR, 1024), jnp.float32),
            pltpu.VMEM((SLICES, SR, 1024), jnp.float32),
            pltpu.VMEM((64, 1024), jnp.bfloat16),
            pltpu.SemaphoreType.DMA((N_SEM,)),
            pltpu.SemaphoreType.DMA((N_SEM,)),
            pltpu.SemaphoreType.DMA((3,)),
        ],
        compiler_params=pltpu.CompilerParams(
            collective_id=0, has_side_effects=True, vmem_limit_bytes=48 * 2**20
        ),
    )(tokens, cotangent, master, moment, second)
    return (*out[:3], out[3].reshape(4096, 1024))


def solution(mesh):
    placed = (
        P(("node", "local"), None),
        P(("node", "local"), None),
        P("node", "local"),
        P("node", "local"),
        P("node", "local"),
    )
    return jax.shard_map(
        on_device,
        mesh=mesh,
        in_specs=placed,
        out_specs=(P("node", "local"), P("node", "local"), P("node", "local"), P(None, "local")),
        check_vma=False,
    )
```

```python
import functools

import jax
import jax.numpy as jnp
from jax import lax
from jax.experimental import pallas as pl
from jax.experimental.pallas import tpu as pltpu
from jax.sharding import PartitionSpec as P

MESH = pl.DeviceIdType.MESH

first_beta = 0.9
second_beta = 0.95
learn_rate = 0.01
decay_rate = 0.1
epsilon = 1e-08
first_fix = 1.0 - 0.9**20
second_fix = 1.0 - 0.95**20

PIECES = 2
WIDTH = 1024 // PIECES
PARTS = 2
SR = 64 // PARTS
SLICES = PIECES * PARTS
STEP, HOP = 1.4, 4.5
TIMES = (6.0, 14.0, 18.0, 24.0, 30.0, 1.0, 1.0)


def kernel(
    tok, cot, master, moment, second,
    master_new, moment_new, second_new, weights,
    tg, cg, part, core_in, z_in, grad, state, ssem, rsem, lsem,
):
    fetch = [
        pltpu.make_async_copy(ref, state.at[i], lsem.at[2 + i])
        for i, ref in enumerate((master, moment, second))
    ]
    for f in fetch:
        f.start()
    node, l = lax.axis_index("node"), lax.axis_index("local")
    c = node % 2
    y = (node // 2) % 4
    h = (node // 8) % 2
    x = node // 16
    z = h * 4 + l

    def dev(dx=0, dy=0, dz=0, dc=0):
        zz = (z + dz + 8) % 8
        xx, yy, cc = (x + dx + 4) % 4, (y + dy + 4) % 4, (c + dc) % 2
        return (((xx * 2 + zz // 4) * 4 + yy) * 2 + cc, zz % 4)

    count = [0]

    def ids(n=1):
        first = count[0]
        count[0] += n
        return first

    def rcopy(src, dst, sid, to):
        return pltpu.make_async_remote_copy(
            src_ref=src, dst_ref=dst, send_sem=ssem.at[sid], recv_sem=rsem.at[sid],
            device_id=to, device_id_type=MESH,
        )

    sent = []

    def start(cp):
        cp.start()
        sent.append(cp)

    barrier = pltpu.get_barrier_semaphore()
    peers = [dev(dx=d) for d in (1, 2, 3)] + [dev(dy=d) for d in (1, 2, 3)]
    peers += [dev(dz=1), dev(dz=-1), dev(dz=4), dev(dc=1)]
    for p in peers:
        pl.semaphore_signal(barrier, inc=1, device_id=p, device_id_type=MESH)
    pl.semaphore_wait(barrier, len(peers))

    def cols(b):
        return pl.ds(pl.multiple_of(b * 1024, 1024), 1024)

    def slot(buf, ry, rx, lo=0, n=128):
        return buf.at[ry, pl.ds(rx * 128 + lo, n)]

    own_t, own_c = tok.at[:, cols(x)], cot.at[:, cols(y)]
    lt = pltpu.make_async_copy(own_t, slot(tg, 0, 0), lsem.at[0])
    lc = pltpu.make_async_copy(own_c, slot(cg, 0, 0), lsem.at[1])
    lt.start()
    lc.start()
    ta, ca = {}, {}
    for d in (1, 3, 2):
        r = (4 - d) % 4
        ta[r] = rcopy(tok.at[:, cols((x + d) % 4)], slot(tg, 0, r), ids(), dev(dx=d))
        ca[r] = rcopy(cot.at[:, cols((y + d) % 4)], slot(cg, r, 0), ids(), dev(dy=d))
        start(ta[r])
        start(ca[r])
    tp, tm, cp_, cm = {}, {}, {}, {}

    def spread_t(rx):
        src = own_t if rx == 0 else slot(tg, 0, rx)
        tp[rx] = rcopy(src, slot(tg, 3, rx), ids(), dev(dy=1))
        tm[rx] = rcopy(src, slot(tg, 1, rx), ids(), dev(dy=-1))
        start(tp[rx])
        start(tm[rx])

    def spread_c(ry):
        src = own_c if ry == 0 else slot(cg, ry, 0)
        cp_[ry] = rcopy(src, slot(cg, ry, 3), ids(), dev(dx=1))
        cm[ry] = rcopy(src, slot(cg, ry, 1), ids(), dev(dx=-1))
        start(cp_[ry])
        start(cm[ry])

    spread_t(0)
    spread_c(0)
    for r in (3, 1, 2):
        ta[r].wait_recv()
        spread_t(r)
        ca[r].wait_recv()
        spread_c(r)
    tfp, tfm, cfp, cfm = {}, {}, {}, {}
    lt.wait()
    lc.wait()

    def forward(r):
        tp[r].wait_recv()
        tfp[r] = rcopy(slot(tg, 3, r, 0, 64), slot(tg, 2, r, 0, 64), ids(), dev(dy=1))
        start(tfp[r])
        cp_[r].wait_recv()
        cfp[r] = rcopy(slot(cg, r, 3, 0, 64), slot(cg, r, 2, 0, 64), ids(), dev(dx=1))
        start(cfp[r])
        tm[r].wait_recv()
        tfm[r] = rcopy(slot(tg, 1, r, 64, 64), slot(tg, 2, r, 64, 64), ids(), dev(dy=-1))
        start(tfm[r])
        cm[r].wait_recv()
        cfm[r] = rcopy(slot(cg, r, 1, 64, 64), slot(cg, r, 2, 64, 64), ids(), dev(dx=-1))
        start(cfm[r])

    def tile(ry, m, p, first):
        rows, out = pl.ds(pl.multiple_of(m * 256, 256), 256), pl.ds(p * WIDTH, WIDTH)
        got = lax.dot_general(
            tg[ry, :, rows], cg[ry, :, out], (((0,), (0,)), ((), ())),
            preferred_element_type=jnp.float32,
        )
        part[rows, out] = got if first else part[rows, out] + got

    def matmul(ry, first):
        @pl.loop(0, 4)
        def _(m):
            for p in range(PIECES):
                tile(ry, m, p, first)

    forward(0)
    forward(3)
    cfp[0].wait_recv()
    cfm[0].wait_recv()
    matmul(0, True)
    forward(1)
    cfp[3].wait_recv()
    cfm[3].wait_recv()
    forward(2)
    matmul(3, False)
    cfp[1].wait_recv()
    cfm[1].wait_recv()
    matmul(1, False)
    cfp[2].wait_recv()
    cfm[2].wait_recv()
    for r in range(4):
        tfp[r].wait_recv()
        tfm[r].wait_recv()

    core_id = ids(8 * PIECES)

    def block(hh, yy, cc, lo=0, n=64):
        return pl.ds(pl.multiple_of(hh * 512 + yy * 128 + cc * 64 + lo, n), n)

    def wide(p):
        return pl.ds(p * WIDTH, WIDTH)

    def core_copy(hh, yy, p):
        return rcopy(
            part.at[block(hh, yy, 1 - c), wide(p)], core_in.at[hh, yy, :, wide(p)],
            core_id + (p * 2 + hh) * 4 + yy, dev(dc=1),
        )

    events = []

    def at(when, what, place=None):
        events.append((when, len(events), place, what))

    r = (z - y + 8) % 8
    q = r % 4
    end = q == 0
    up = jnp.where(r < 4, 1, 0)
    z_id = [ids(4 * SLICES), ids(4 * SLICES)]
    g_id = ids(4 * SLICES)
    order = ((2, 3, 0, 1), (0, 1, 2, 3))

    for p in range(PIECES):
        for k in range(4):
            half = jnp.where(end, (up, up, 1 - up, 1 - up)[k], (up, 1 - up, up, 1 - up)[k])
            pair = jnp.where(end, (0, 1, 0, 1)[k], (1, 0, 0, 1)[k])
            tile(2, half * 2 + pair, p, False)
            for b in range(2):
                core_copy(half, pair * 2 + b, p).start()

    def chunk(hh, s, yy):
        return block(hh, yy, c, (s % PARTS) * SR, SR), wide(s // PARTS)

    def z_copy(way, hh, s, yy):
        return rcopy(
            part.at[chunk(hh, s, yy)], z_in.at[way, s, yy],
            z_id[way] + s * 4 + yy, dev(dz=1 - 2 * way),
        )

    def g_copy(s, yy):
        return pltpu.make_async_remote_copy(
            src_ref=part.at[chunk(h, s, yy)], dst_ref=grad.at[s],
            send_sem=ssem.at[g_id + s * 4 + yy], recv_sem=rsem.at[g_id + s],
            device_id=(((x * 2 + h) * 4 + yy) * 2 + c, l), device_id_type=MESH,
        )

    def core_sum(hh, yy, p):
        core_copy(hh, yy, p).wait_recv()
        part[block(hh, yy, c), wide(p)] += core_in[hh, yy, :, wide(p)]

    def link(place, way, k):
        hh = up if way == 0 else 1 - up
        s, i = k // 4, k % 4
        yy = order[way][i]
        if s % PARTS == 0:
            core_sum(hh, yy, s // PARTS)
        if i >= 2 or place != (1 if way == 0 else 3):
            z_copy(way, hh, s, yy).wait_recv()
            rows, width = chunk(hh, s, yy)
            part[rows, width] += z_in[way, s, yy]
        z_copy(way, hh, s, yy).start()

    for place in (1, 2, 3):
        for way in range(2):
            for k in range(4 * SLICES):
                behind = place - 1 if way == 0 else 3 - place
                at(k * STEP + HOP * behind, functools.partial(link, place, way, k), place)

    def far(s, i, way):
        yy = order[way][i + 2]
        if s % PARTS == 0:
            core_sum(up, yy, s // PARTS)
        z_copy(way, up, s, yy).start()

    def last(s, yy):
        if s % PARTS == 0:
            core_sum(h, yy, s // PARTS)
        z_copy(0, h, s, yy).wait_recv()
        z_copy(1, h, s, yy).wait_recv()
        rows, width = chunk(h, s, yy)
        total = part[rows, width] + (z_in[0, s, yy] + z_in[1, s, yy])
        part[rows, width] = total

        @pl.when(yy == y)
        def _():
            grad[s] = total

        @pl.when(yy != y)
        def _():
            g_copy(s, yy).start()

    for s in range(SLICES):
        for i in range(2):
            for way in range(2):
                at(0 if s < PARTS else s * 2 * STEP, functools.partial(far, s, i, way), 0)
        for yy in range(4):
            at((s * 4 + yy) * STEP + 3 * HOP + 1, functools.partial(last, s, yy), 0)

    def adam(s):
        if s == 0:
            for f in fetch:
                f.wait()

        @pl.when(jnp.logical_not(end))
        def _():
            g_copy(s, 0).wait_recv()

        rows, width = pl.ds((s % PARTS) * SR, SR), wide(s // PARTS)
        g = grad[s]
        old = state[0, rows, width]
        m_new = first_beta * state[1, rows, width] + (1.0 - first_beta) * g
        s_new = second_beta * state[2, rows, width] + (1.0 - second_beta) * g * g
        update = m_new / first_fix / (jnp.sqrt(s_new / second_fix) + epsilon) + decay_rate * old
        new = old - learn_rate * update
        master_new[rows, width] = new
        moment_new[rows, width] = m_new
        second_new[rows, width] = s_new
        weights[x, h, y, c, rows, width] = new.astype(jnp.bfloat16)

    def da(d):
        return dev(dx=d * (1 - c), dy=d * c)

    def db(d):
        return dev(dx=d * c, dy=d * (1 - c))

    both = slice(None)
    side = dev(dc=1)
    side_id = ids()

    def spread(p):
        def unit(hh, a=0, b=0):
            xx = (x + a * (1 - c) + b * c + 4) % 4
            yy = (y + a * c + b * (1 - c) + 4) % 4
            return weights.at[xx, hh, yy, c, :, wide(p)]

        def pass_on(ref, to):
            cp = rcopy(ref, ref, ids(), to)
            start(cp)
            return cp

        def to_side(hh, a=0, b=0):
            rcopy(unit(hh, a, b), unit(hh, a, b), side_id, side).start()

        w_a, w_b, f_b, w_z = {}, {}, {}, {}

        def a_send(k):
            hh = (h, 1 - h)[k]
            for d in (1, -1, 2):
                w_a[k, d] = pass_on(unit(hh), da(d))

        def b_send(a, k, hh):
            for d in (1, -1):
                w_b[a, k, d] = pass_on(unit(hh, a), db(d))

        def first():
            for s in range(p * PARTS, (p + 1) * PARTS):
                adam(s)
            w_z[0] = pass_on(unit(h), dev(dz=4))
            a_send(0)
            b_send(0, 0, h)
            to_side(h)

        def second():
            w_z[0].wait_recv()
            a_send(1)
            b_send(0, 1, 1 - h)
            to_side(1 - h)

        def third(a):
            for k in range(2):
                w_a[k, 2 if a == 2 else -a].wait_recv()
            b_send(a, 0, both)
            to_side(both, a)

        def onward(a, d):
            for k in range(2 if a == 0 else 1):
                w_b[a, k, d].wait_recv()
            hh = h if d == 1 else 1 - h
            f_b[a, d] = pass_on(unit(hh, a, -d), db(d))
            to_side(both, a, -d)

        def finish(a):
            f_b[a, 1].wait_recv()
            f_b[a, -1].wait_recv()
            to_side(both, a, 2)

        P_ = functools.partial
        T = TIMES
        out = [(T[0], first), (T[1], second)]
        for i, a in enumerate((-1, 1, 2)):
            out.append((T[2] + i * T[5], P_(third, a)))
        for i, a in enumerate((0, -1, 1, 2)):
            for d in (1, -1):
                out.append((T[3] + i * T[6], P_(onward, a, d)))
            out.append((T[4] + i * T[6], P_(finish, a)))
        return out

    for p in range(PIECES):
        ready = (p + 1) * 4 * PARTS * STEP + 3 * HOP + 1
        for when, stage in spread(p):
            at(ready + when, stage)

    events.sort(key=lambda e: e[:2])
    slots = sorted({int(e[0]) for e in events})
    for slot_ in slots:
        now = [e for e in events if int(e[0]) == slot_]
        for place in range(4):
            todo = [e[3] for e in now if e[2] == place]
            if todo:
                @pl.when(q == place)
                def _():
                    for what in todo:
                        what()
        for e in now:
            if e[2] is None:
                e[3]()

    all_side = rcopy(weights.at[:, :, :, c], weights.at[:, :, :, 1 - c], side_id, side)
    all_side.wait_recv()
    all_side.wait_send()
    assert count[0] == N_SEM, count[0]
    for cp in sent:
        cp.wait_send()
    for p in range(PIECES):
        for b in range(8):
            core_copy(b // 4, b % 4, p).wait_send()

    @pl.when(jnp.logical_not(end))
    def _():
        for s in range(SLICES):
            for yy in range(4):
                for way in range(2):
                    z_copy(way, 0, s, yy).wait_send()

    @pl.when(end)
    def _():
        for s in range(SLICES):
            for i in range(2):
                for way in range(2):
                    z_copy(way, up, s, order[way][i + 2]).wait_send()
            for yy in range(4):
                @pl.when(yy != y)
                def _():
                    g_copy(s, yy).wait_send()


def copy_kernel(*refs):
    sem = refs[-1]
    copies = [pltpu.make_async_copy(refs[i], refs[4 + i], sem.at[i]) for i in (3, 0, 1, 2)]
    for cp in copies:
        cp.start()
    for cp in copies:
        cp.wait()


def write_out(*arrays):
    return pl.pallas_call(
        copy_kernel,
        out_shape=[jax.ShapeDtypeStruct(a.shape, a.dtype) for a in arrays],
        in_specs=[pl.BlockSpec(memory_space=pltpu.VMEM)] * 4,
        out_specs=[pl.BlockSpec(memory_space=pltpu.HBM)] * 4,
        scratch_shapes=[pltpu.SemaphoreType.DMA((4,))],
        compiler_params=pltpu.CompilerParams(vmem_limit_bytes=2**20),
    )(*arrays)


N_SEM = 153
VMEM_GRANT = 36 * 2**20


def on_device(tokens, cotangent, master, moment, second):
    vmem, hbm = pl.BlockSpec(memory_space=pltpu.VMEM), pl.BlockSpec(memory_space=pl.ANY)
    f32 = jax.ShapeDtypeStruct((64, 1024), jnp.float32)
    out = pl.pallas_call(
        kernel,
        out_shape=(f32, f32, f32, jax.ShapeDtypeStruct((4, 2, 4, 2, 64, 1024), jnp.bfloat16)),
        in_specs=[hbm] * 5,
        out_specs=(vmem, vmem, vmem, vmem),
        scratch_shapes=[
            pltpu.VMEM((4, 512, 1024), jnp.bfloat16),
            pltpu.VMEM((4, 512, 1024), jnp.bfloat16),
            pltpu.VMEM((1024, 1024), jnp.float32),
            pltpu.VMEM((2, 4, 64, 1024), jnp.float32),
            pltpu.VMEM((2, SLICES, 4, SR, WIDTH), jnp.float32),
            pltpu.VMEM((SLICES, SR, WIDTH), jnp.float32),
            pltpu.VMEM((3, 64, 1024), jnp.float32),
            pltpu.SemaphoreType.DMA((N_SEM,)),
            pltpu.SemaphoreType.DMA((N_SEM,)),
            pltpu.SemaphoreType.DMA((5,)),
        ],
        compiler_params=pltpu.CompilerParams(
            collective_id=0, has_side_effects=True, vmem_limit_bytes=VMEM_GRANT
        ),
    )(tokens, cotangent, master, moment, second)
    return write_out(*out[:3], out[3].reshape(4096, 1024))


def solution(mesh):
    placed = (
        P(("node", "local"), None),
        P(("node", "local"), None),
        P("node", "local"),
        P("node", "local"),
        P("node", "local"),
    )
    return jax.shard_map(
        on_device,
        mesh=mesh,
        in_specs=placed,
        out_specs=(P("node", "local"), P("node", "local"), P("node", "local"), P(None, "local")),
        check_vma=False,
    )
```

```python
import functools

import jax
import jax.numpy as jnp
from jax import lax
from jax.experimental import pallas as pl
from jax.experimental.pallas import tpu as pltpu
from jax.sharding import PartitionSpec as P

MESH = pl.DeviceIdType.MESH

first_beta = 0.9
second_beta = 0.95
learn_rate = 0.01
decay_rate = 0.1
epsilon = 1e-08
first_fix = 1.0 - 0.9**20
second_fix = 1.0 - 0.95**20

PIECES = 2
WIDTH = 1024 // PIECES
PARTS = 2
SR = 64 // PARTS
SLICES = PIECES * PARTS
QUADS = ((0, 0), (1, 0), (0, 1), (1, 1))
GATHER = (
    (0, 4, 5, 7, 9, 13, 16, 19, 20, 22, 23, 26),
    (14, 24, 25, 27, 31, 35, 38, 41, 42, 44, 45, 49),
)
CHAIN = (33, 52, 57.6, 63.2)
STEP, HOP = 1.4, 4.5
TIMES = (6.0, 14.0, 11.0, 20.0, 16.0, 25.0, 31.0, 1.0)


def kernel(
    tok, cot, master, moment, second,
    master_new, moment_new, second_new, weights,
    tg, cg, part, core_in, z_in, grad, state, ssem, rsem, lsem,
):
    fetch = [
        pltpu.make_async_copy(ref, state.at[i], lsem.at[6 + i])
        for i, ref in enumerate((master, moment, second))
    ]
    for f in fetch:
        f.start()
    node, l = lax.axis_index("node"), lax.axis_index("local")
    c = lax.rem(node, 2)
    y = lax.rem(lax.div(node, 2), 4)
    h = lax.rem(lax.div(node, 8), 2)
    x = lax.div(node, 16)
    z = h * 4 + l

    def around(v, n):
        return [v] + [lax.rem(v + d, n) for d in range(1, n)]

    xs, ys, zs = around(x, 4), around(y, 4), around(z, 8)

    def node_of(xx, hh, yy, cc):
        return ((xx * 2 + hh) * 4 + yy) * 2 + cc

    peer = {("x", d): (node_of(xs[d], h, y, c), l) for d in (1, 2, 3)}
    peer |= {("y", d): (node_of(x, h, ys[d], c), l) for d in (1, 2, 3)}
    peer |= {("z", d): (node_of(x, lax.div(zs[d], 4), y, c), lax.rem(zs[d], 4)) for d in (1, 7, 4)}
    peer["core", 1] = (node_of(x, h, y, 1 - c), l)
    for d in (1, 2, 3):
        for axis, one, two in (("a", "x", "y"), ("b", "y", "x")):
            peer[axis, d] = (jnp.where(c == 0, peer[one, d][0], peer[two, d][0]), l)
    row_peer = [(node_of(x, h, yy, c), l) for yy in range(4)]
    place_of = {
        (a, b): (jnp.where(c == 0, xs[a % 4], xs[b % 4]), jnp.where(c == 0, ys[b % 4], ys[a % 4]))
        for a in (0, -1, 1, 2) for b in (0, -1, 1, 2)
    }

    def dev(dx=0, dy=0, dz=0, dc=0):
        if dx:
            return peer["x", dx % 4]
        if dy:
            return peer["y", dy % 4]
        return peer["z", dz % 8] if dz else peer["core", dc]

    count = [0]

    def ids(n=1):
        first = count[0]
        count[0] += n
        return first

    CORE, CHAIN_Z, ROW, WEIGHTS, SIDE = range(2, 7)

    def rcopy(kind, src, dst, sid, to):
        return pltpu.make_async_remote_copy(
            src_ref=src, dst_ref=dst, send_sem=ssem.at[kind], recv_sem=rsem.at[sid],
            device_id=to, device_id_type=MESH,
        )

    def all_sent(kind, kib):
        rows = part.at[pl.ds(0, kib // 4)]
        rcopy(kind, rows, rows, 0, dev(dc=1)).wait_send()

    barrier = pltpu.get_barrier_semaphore()
    peers = [dev(dx=d) for d in (1, 2, 3)] + [dev(dy=d) for d in (1, 2, 3)]
    peers += [dev(dz=1), dev(dz=-1), dev(dz=4), dev(dc=1)]
    for p in peers:
        pl.semaphore_signal(barrier, inc=1, device_id=p, device_id_type=MESH)
    pl.semaphore_wait(barrier, len(peers))

    events = []

    def at(when, what, place=None):
        events.append((when, len(events), place, what))

    def slot(buf, u, ry, rx, lo=0, n=128):
        return buf.at[u, ry, pl.ds(rx * 128 + lo, n)]

    def t_cols(b, hh, u):
        return tok.at[:, pl.ds(pl.multiple_of(b * 1024 + hh * 512 + u * 256, 256), 256)]

    def c_cols(b, u):
        return cot.at[:, pl.ds(pl.multiple_of(b * 1024 + u * 512, 512), 512)]

    ta, ca, tp, tm, cp_, cm, tfp, tfm, cfp, cfm = ({} for _ in range(10))

    def spread_t(u, r):
        src = slot(tg, u, 0, r)
        tp[u, r] = rcopy(u, src, slot(tg, u, 3, r), ids(), dev(dy=1))
        tm[u, r] = rcopy(u, src, slot(tg, u, 1, r), ids(), dev(dy=-1))
        tp[u, r].start()
        tm[u, r].start()

    def spread_c(u, r):
        src = c_cols(y, u) if r == 0 else slot(cg, u, r, 0)
        cp_[u, r] = rcopy(u, src, slot(cg, u, r, 3), ids(), dev(dx=1))
        cm[u, r] = rcopy(u, src, slot(cg, u, r, 1), ids(), dev(dx=-1))
        cp_[u, r].start()
        cm[u, r].start()

    def gather_first(u):
        own = [
            pltpu.make_async_copy(
                t_cols(x, hh, u), tg.at[u, 0, pl.ds(0, 128), pl.ds(hh * 256, 256)], lsem.at[3 * u + hh]
            )
            for hh in range(2)
        ]
        own.append(pltpu.make_async_copy(c_cols(y, u), slot(cg, u, 0, 0), lsem.at[3 * u + 2]))
        for cp in own:
            cp.start()
        for d in (1, 3, 2):
            r = (4 - d) % 4
            ta[u, r] = rcopy(u, slot(tg, u, 0, r), slot(tg, u, 0, r), ids(), dev(dx=d))
            for hh in range(2):
                rcopy(u,
                    t_cols(xs[d], hh, u), tg.at[u, 0, pl.ds(r * 128, 128), pl.ds(hh * 256, 256)],
                    count[0] - 1, dev(dx=d),
                ).start()
            ca[u, r] = rcopy(u, c_cols(ys[d], u), slot(cg, u, r, 0), ids(), dev(dy=d))
            ca[u, r].start()
        spread_c(u, 0)
        for cp in own:
            cp.wait()
        spread_t(u, 0)

    def gather_next(u, r):
        ta[u, r].wait_recv()
        spread_t(u, r)
        ca[u, r].wait_recv()
        spread_c(u, r)

    def forward(u, r):
        tp[u, r].wait_recv()
        tfp[u, r] = rcopy(u, slot(tg, u, 3, r, 0, 64), slot(tg, u, 2, r, 0, 64), ids(), dev(dy=1))
        tfp[u, r].start()
        cp_[u, r].wait_recv()
        cfp[u, r] = rcopy(u, slot(cg, u, r, 3, 0, 64), slot(cg, u, r, 2, 0, 64), ids(), dev(dx=1))
        cfp[u, r].start()
        tm[u, r].wait_recv()
        tfm[u, r] = rcopy(u, slot(tg, u, 1, r, 64, 64), slot(tg, u, 2, r, 64, 64), ids(), dev(dy=-1))
        tfm[u, r].start()
        cm[u, r].wait_recv()
        cfm[u, r] = rcopy(u, slot(cg, u, r, 1, 64, 64), slot(cg, u, r, 2, 64, 64), ids(), dev(dx=-1))
        cfm[u, r].start()

    def tile(u, p, ry, hh):
        rows = pl.ds(pl.multiple_of(hh * 512 + u * 256, 256), 256)
        cols = pl.ds(pl.multiple_of(hh * 256, 256), 256)
        got = lax.dot_general(
            tg[u, ry, :, cols], cg[p, ry], (((0,), (0,)), ((), ())),
            preferred_element_type=jnp.float32,
        )
        part[rows, wide(p)] = got if ry == 0 else part[rows, wide(p)] + got

    def product(half, ry):
        cfp[half, ry].wait_recv()
        cfm[half, ry].wait_recv()
        for u, p in QUADS[:1] if half == 0 else QUADS[1:]:
            @pl.loop(0, 2)
            def _(hh):
                tile(u, p, ry, hh)

    def product_last(half):
        cfp[half, 2].wait_recv()
        cfm[half, 2].wait_recv()
        for r in range(4):
            tfp[half, r].wait_recv()
            tfm[half, r].wait_recv()
        for u, p in QUADS[:1] if half == 0 else QUADS[1:]:
            for hh in (up, 1 - up):
                tile(u, p, 2, hh)
                for yy in (2 * u, 2 * u + 1):
                    core_copy(hh, yy, p).start()

    for u in range(2):
        G = GATHER[u]
        at(G[0], functools.partial(gather_first, u))
        for i, r in enumerate((3, 1, 2)):
            at(G[1 + i], functools.partial(gather_next, u, r))
        for i, r in enumerate((0, 3, 1, 2)):
            at(G[4 + i], functools.partial(forward, u, r))
        for i, r in enumerate((0, 3, 1)):
            at(G[8 + i], functools.partial(product, u, r))
        at(G[11], functools.partial(product_last, u))

    core_id = ids(8 * PIECES)

    def block(hh, yy, cc, lo=0, n=64):
        return pl.ds(pl.multiple_of(hh * 512 + yy * 128 + cc * 64 + lo, n), n)

    def wide(p):
        return pl.ds(p * WIDTH, WIDTH)

    def core_copy(hh, yy, p):
        return rcopy(
            CORE, part.at[block(hh, yy, 1 - c), wide(p)], core_in.at[hh, yy, :, wide(p)],
            core_id + (p * 2 + hh) * 4 + yy, dev(dc=1),
        )

    r = lax.rem(z - y + 8, 8)
    q = lax.rem(r, 4)
    end = q == 0
    up = jnp.where(r < 4, 1, 0)
    z_id = [ids(4 * SLICES), ids(4 * SLICES)]
    g_id = ids(SLICES)

    def chunk(hh, s, yy):
        return block(hh, yy, c, (s % PARTS) * SR, SR), wide(s // PARTS)

    def z_copy(way, hh, s, yy):
        return rcopy(
            CHAIN_Z, part.at[chunk(hh, s, yy)], z_in.at[way, s, yy],
            z_id[way] + s * 4 + yy, dev(dz=1 - 2 * way),
        )

    def g_copy(s, yy):
        return pltpu.make_async_remote_copy(
            src_ref=part.at[chunk(h, s, yy)], dst_ref=grad.at[s],
            send_sem=ssem.at[ROW], recv_sem=rsem.at[g_id + s],
            device_id=row_peer[yy], device_id_type=MESH,
        )

    def core_sum(hh, yy, p):
        core_copy(hh, yy, p).wait_recv()
        part[block(hh, yy, c), wide(p)] += core_in[hh, yy, :, wide(p)]

    def parts_of(j, way):
        u, p = QUADS[j]
        return [(p * PARTS + s, 2 * u + (i + 1 - way) % 2) for s in range(PARTS) for i in range(2)]

    def link(place, way, j, i):
        hh = up if way == 0 else 1 - up
        s, yy = parts_of(j, way)[i]
        if s % PARTS == 0:
            core_sum(hh, yy, s // PARTS)
        if i % 2 or place != (1 if way == 0 else 3):
            z_copy(way, hh, s, yy).wait_recv()
            rows, width = chunk(hh, s, yy)
            part[rows, width] += z_in[way, s, yy]
        z_copy(way, hh, s, yy).start()

    def far(j, i, way):
        s, yy = parts_of(j, way)[i]
        if s % PARTS == 0:
            core_sum(up, yy, s // PARTS)
        z_copy(way, up, s, yy).start()

    def last(s, yy):
        if s % PARTS == 0:
            core_sum(h, yy, s // PARTS)
        z_copy(0, h, s, yy).wait_recv()
        z_copy(1, h, s, yy).wait_recv()
        rows, width = chunk(h, s, yy)
        total = part[rows, width] + (z_in[0, s, yy] + z_in[1, s, yy])
        part[rows, width] = total

        @pl.when(yy == y)
        def _():
            grad[s] = total

        @pl.when(yy != y)
        def _():
            g_copy(s, yy).start()

    for j in range(4):
        for i in range(2 * PARTS):
            for way in range(2):
                for place in (1, 2, 3):
                    behind = place - 1 if way == 0 else 3 - place
                    at(CHAIN[j] + i * STEP + HOP * behind, functools.partial(link, place, way, j, i), place)
                if i % 2:
                    at(CHAIN[j] + i * STEP - STEP, functools.partial(far, j, i, way), 0)
            at(CHAIN[j] + i * STEP + 3 * HOP + 1, functools.partial(last, *parts_of(j, 1)[i]), 0)

    def adam(s):
        if s == 0:
            for f in fetch:
                f.wait()

        @pl.when(jnp.logical_not(end))
        def _():
            g_copy(s, 0).wait_recv()

        rows, width = pl.ds((s % PARTS) * SR, SR), wide(s // PARTS)
        g = grad[s]
        old = state[0, rows, width]
        m_new = first_beta * state[1, rows, width] + (1.0 - first_beta) * g
        s_new = second_beta * state[2, rows, width] + (1.0 - second_beta) * g * g
        update = m_new / first_fix / (jnp.sqrt(s_new / second_fix) + epsilon) + decay_rate * old
        new = old - learn_rate * update
        master_new[rows, width] = new
        moment_new[rows, width] = m_new
        second_new[rows, width] = s_new
        weights[x, h, y, c, rows, width] = new.astype(jnp.bfloat16)

    def da(d):
        return peer["a", d % 4]

    def db(d):
        return peer["b", d % 4]

    both = slice(None)
    side = dev(dc=1)
    side_id = ids()

    def spread(p):
        def unit(hh, a=0, b=0):
            xx, yy = place_of[a, b]
            return weights.at[xx, hh, yy, c, :, wide(p)]

        def pass_on(ref, to):
            cp = rcopy(WEIGHTS, ref, ref, ids(), to)
            cp.start()
            return cp

        def to_side(hh, a=0, b=0):
            rcopy(SIDE, unit(hh, a, b), unit(hh, a, b), side_id, side).start()

        w_a, w_b, f_b, w_z = {}, {}, {}, {}

        def a_send(k):
            hh = (h, 1 - h)[k]
            for d in (1, -1, 2):
                w_a[k, d] = pass_on(unit(hh), da(d))

        def b_send(a, k, hh):
            for d in (1, -1):
                w_b[a, k, d] = pass_on(unit(hh, a), db(d))

        def first():
            for s in range(p * PARTS, (p + 1) * PARTS):
                adam(s)
            w_z[0] = pass_on(unit(h), dev(dz=4))
            a_send(0)
            b_send(0, 0, h)
            to_side(h)

        def second():
            w_z[0].wait_recv()
            a_send(1)
            b_send(0, 1, 1 - h)
            to_side(1 - h)

        def third(a, k):
            w_a[k, 2 if a == 2 else -a].wait_recv()
            b_send(a, k, (h, 1 - h)[k])
            if k == 1:
                to_side(both, a)

        def onward(a, k):
            d = (1, -1)[k]
            w_b[a, k, d].wait_recv()
            ref = unit((h, 1 - h)[k], a, -d)
            f_b[a, d] = pass_on(ref, db(d))
            if k == 1:
                w_b[a, 0, -1].wait_recv()
                to_side(both, a, 1)
                w_b[a, 1, 1].wait_recv()
                to_side(both, a, -1)

        def finish(a):
            f_b[a, 1].wait_recv()
            f_b[a, -1].wait_recv()
            to_side(both, a, 2)

        P_ = functools.partial
        T = TIMES
        out = [(T[0], first), (T[1], second)]
        for k in range(2):
            for i, a in enumerate((-1, 1, 2)):
                out.append((T[2 + k] + i * T[7], P_(third, a, k)))
            for i, a in enumerate((0, -1, 1, 2)):
                out.append((T[4 + k] + i * T[7], P_(onward, a, k)))
        for i, a in enumerate((0, -1, 1, 2)):
            out.append((T[6] + i * T[7], P_(finish, a)))
        return out

    for p in range(PIECES):
        ready = CHAIN[2 * p + 1] + 2 * PARTS * STEP + 3 * HOP + 1
        for when, stage in spread(p):
            at(ready + when, stage)

    events.sort(key=lambda e: e[:2])
    slots = sorted({int(e[0]) for e in events})
    for slot_ in slots:
        now = [e for e in events if int(e[0]) == slot_]
        for place in range(4):
            todo = [e[3] for e in now if e[2] == place]
            if todo:
                @pl.when(q == place)
                def _():
                    for what in todo:
                        what()
        for e in now:
            if e[2] is None:
                e[3]()

    all_side = rcopy(SIDE, weights.at[:, :, :, c], weights.at[:, :, :, 1 - c], side_id, side)
    all_side.wait_recv()
    all_side.wait_send()
    assert count[0] == N_SEM, count[0]
    for u in range(2):
        all_sent(u, 6 * 128 + 16 * 128 + 16 * 64)
    all_sent(CORE, 16 * 128)
    all_sent(WEIGHTS, 62 * 64)

    @pl.when(jnp.logical_not(end))
    def _():
        all_sent(CHAIN_Z, 32 * 64)

    @pl.when(end)
    def _():
        all_sent(CHAIN_Z, 16 * 64)
        all_sent(ROW, 12 * 64)


def copy_kernel(*refs):
    sem = refs[-1]
    copies = [pltpu.make_async_copy(refs[i], refs[4 + i], sem.at[i]) for i in (3, 0, 1, 2)]
    for cp in copies:
        cp.start()
    for cp in copies:
        cp.wait()


def write_out(*arrays):
    return pl.pallas_call(
        copy_kernel,
        out_shape=[jax.ShapeDtypeStruct(a.shape, a.dtype) for a in arrays],
        in_specs=[pl.BlockSpec(memory_space=pltpu.VMEM)] * 4,
        out_specs=[pl.BlockSpec(memory_space=pltpu.HBM)] * 4,
        scratch_shapes=[pltpu.SemaphoreType.DMA((4,))],
        compiler_params=pltpu.CompilerParams(vmem_limit_bytes=2**20),
    )(*arrays)


N_SEM = 191
VMEM_GRANT = 36 * 2**20


def on_device(tokens, cotangent, master, moment, second):
    vmem, hbm = pl.BlockSpec(memory_space=pltpu.VMEM), pl.BlockSpec(memory_space=pl.ANY)
    f32 = jax.ShapeDtypeStruct((64, 1024), jnp.float32)
    out = pl.pallas_call(
        kernel,
        out_shape=(f32, f32, f32, jax.ShapeDtypeStruct((4, 2, 4, 2, 64, 1024), jnp.bfloat16)),
        in_specs=[hbm] * 5,
        out_specs=(vmem, vmem, vmem, vmem),
        scratch_shapes=[
            pltpu.VMEM((2, 4, 512, 512), jnp.bfloat16),
            pltpu.VMEM((2, 4, 512, 512), jnp.bfloat16),
            pltpu.VMEM((1024, 1024), jnp.float32),
            pltpu.VMEM((2, 4, 64, 1024), jnp.float32),
            pltpu.VMEM((2, SLICES, 4, SR, WIDTH), jnp.float32),
            pltpu.VMEM((SLICES, SR, WIDTH), jnp.float32),
            pltpu.VMEM((3, 64, 1024), jnp.float32),
            pltpu.SemaphoreType.DMA((7,)),
            pltpu.SemaphoreType.DMA((N_SEM,)),
            pltpu.SemaphoreType.DMA((9,)),
        ],
        compiler_params=pltpu.CompilerParams(
            collective_id=0, has_side_effects=True, vmem_limit_bytes=VMEM_GRANT
        ),
    )(tokens, cotangent, master, moment, second)
    return write_out(*out[:3], out[3].reshape(4096, 1024))


def solution(mesh):
    placed = (
        P(("node", "local"), None),
        P(("node", "local"), None),
        P("node", "local"),
        P("node", "local"),
        P("node", "local"),
    )
    return jax.shard_map(
        on_device,
        mesh=mesh,
        in_specs=placed,
        out_specs=(P("node", "local"), P("node", "local"), P("node", "local"), P(None, "local")),
        check_vma=False,
    )
```

```python
import functools

import jax
import jax.numpy as jnp
from jax import lax
from jax.experimental import pallas as pl
from jax.experimental.pallas import tpu as pltpu
from jax.sharding import PartitionSpec as P

MESH = pl.DeviceIdType.MESH

first_beta = 0.9
second_beta = 0.95
learn_rate = 0.01
decay_rate = 0.1
epsilon = 1e-08
first_fix = 1.0 - 0.9**20
second_fix = 1.0 - 0.95**20

PIECES = 2
WIDTH = 1024 // PIECES
PARTS = 4
SR = 64 // PARTS
SLICES = PIECES * PARTS
QUADS = ((0, 0), (1, 0), (0, 1), (1, 1))
GATHER = (
    (0, 4, 5, 7, 9, 13, 16, 19, 20, 22, 23, 26),
    (14, 24, 25, 27, 31, 35, 38, 41, 42, 44, 45, 49),
)
CHAIN = (33, 52, 57.6, 63.2)
STEP, HOP = 0.7, 5.2
TIMES = (6.0, 14.0, 11.0, 20.0, 16.0, 25.0, 31.0, 1.0)


def kernel(
    tok, cot, master, moment, second,
    master_new, moment_new, second_new, weights,
    tg, cg, part, core_in, z_in, grad, state, ssem, rsem, lsem,
):
    fetch = [
        pltpu.make_async_copy(ref, state.at[i], lsem.at[6 + i])
        for i, ref in enumerate((master, moment, second))
    ]
    for f in fetch:
        f.start()
    node, l = lax.axis_index("node"), lax.axis_index("local")
    c = lax.rem(node, 2)
    y = lax.rem(lax.div(node, 2), 4)
    h = lax.rem(lax.div(node, 8), 2)
    x = lax.div(node, 16)
    z = h * 4 + l

    def around(v, n):
        return [v] + [lax.rem(v + d, n) for d in range(1, n)]

    xs, ys, zs = around(x, 4), around(y, 4), around(z, 8)

    def node_of(xx, hh, yy, cc):
        return ((xx * 2 + hh) * 4 + yy) * 2 + cc

    peer = {("x", d): (node_of(xs[d], h, y, c), l) for d in (1, 2, 3)}
    peer |= {("y", d): (node_of(x, h, ys[d], c), l) for d in (1, 2, 3)}
    peer |= {("z", d): (node_of(x, lax.div(zs[d], 4), y, c), lax.rem(zs[d], 4)) for d in (1, 7, 4)}
    peer["core", 1] = (node_of(x, h, y, 1 - c), l)
    for d in (1, 2, 3):
        for axis, one, two in (("a", "x", "y"), ("b", "y", "x")):
            peer[axis, d] = (jnp.where(c == 0, peer[one, d][0], peer[two, d][0]), l)
    row_peer = [(node_of(x, h, yy, c), l) for yy in range(4)]
    place_of = {
        (a, b): (jnp.where(c == 0, xs[a % 4], xs[b % 4]), jnp.where(c == 0, ys[b % 4], ys[a % 4]))
        for a in (0, -1, 1, 2) for b in (0, -1, 1, 2)
    }

    def dev(dx=0, dy=0, dz=0, dc=0):
        if dx:
            return peer["x", dx % 4]
        if dy:
            return peer["y", dy % 4]
        return peer["z", dz % 8] if dz else peer["core", dc]

    count = [0]

    def ids(n=1):
        first = count[0]
        count[0] += n
        return first

    CORE, CHAIN_Z, ROW, WEIGHTS, SIDE = range(2, 7)

    def rcopy(kind, src, dst, sid, to):
        return pltpu.make_async_remote_copy(
            src_ref=src, dst_ref=dst, send_sem=ssem.at[kind], recv_sem=rsem.at[sid],
            device_id=to, device_id_type=MESH,
        )

    def all_sent(kind, kib):
        rows = part.at[pl.ds(0, kib // 4)]
        rcopy(kind, rows, rows, 0, dev(dc=1)).wait_send()

    barrier = pltpu.get_barrier_semaphore()
    peers = [dev(dx=d) for d in (1, 2, 3)] + [dev(dy=d) for d in (1, 2, 3)]
    peers += [dev(dz=1), dev(dz=-1), dev(dz=4), dev(dc=1)]
    for p in peers:
        pl.semaphore_signal(barrier, inc=1, device_id=p, device_id_type=MESH)
    pl.semaphore_wait(barrier, len(peers))

    events = []

    def at(when, what, place=None):
        events.append((when, len(events), place, what))

    def slot(buf, u, ry, rx, lo=0, n=128):
        return buf.at[u, ry, pl.ds(rx * 128 + lo, n)]

    def t_cols(b, hh, u):
        return tok.at[:, pl.ds(pl.multiple_of(b * 1024 + hh * 512 + u * 256, 256), 256)]

    def c_cols(b, u):
        return cot.at[:, pl.ds(pl.multiple_of(b * 1024 + u * 512, 512), 512)]

    ta, ca, tp, tm, cp_, cm, tf, cf = ({} for _ in range(8))

    def spread_t(u, r):
        src = slot(tg, u, 0, r)
        tp[u, r] = rcopy(u, src, slot(tg, u, 3, r), ids(), dev(dy=1))
        tm[u, r] = rcopy(u, src, slot(tg, u, 1, r), ids(), dev(dy=-1))
        tp[u, r].start()
        tm[u, r].start()

    def spread_c(u, r):
        src = c_cols(y, u) if r == 0 else slot(cg, u, r, 0)
        cp_[u, r] = rcopy(u, src, slot(cg, u, r, 3), ids(), dev(dx=1))
        cm[u, r] = rcopy(u, src, slot(cg, u, r, 1), ids(), dev(dx=-1))
        cp_[u, r].start()
        cm[u, r].start()

    def gather_first(u):
        own = [
            pltpu.make_async_copy(
                t_cols(x, hh, u), tg.at[u, 0, pl.ds(0, 128), pl.ds(hh * 256, 256)], lsem.at[3 * u + hh]
            )
            for hh in range(2)
        ]
        own.append(pltpu.make_async_copy(c_cols(y, u), slot(cg, u, 0, 0), lsem.at[3 * u + 2]))
        for cp in own:
            cp.start()
        for d in (1, 3, 2):
            r = (4 - d) % 4
            ta[u, r] = rcopy(u, slot(tg, u, 0, r), slot(tg, u, 0, r), ids(), dev(dx=d))
            for hh in range(2):
                rcopy(u,
                    t_cols(xs[d], hh, u), tg.at[u, 0, pl.ds(r * 128, 128), pl.ds(hh * 256, 256)],
                    count[0] - 1, dev(dx=d),
                ).start()
            ca[u, r] = rcopy(u, c_cols(ys[d], u), slot(cg, u, r, 0), ids(), dev(dy=d))
            ca[u, r].start()
        spread_c(u, 0)
        for cp in own:
            cp.wait()
        spread_t(u, 0)

    def gather_next(u, r):
        ta[u, r].wait_recv()
        spread_t(u, r)
        ca[u, r].wait_recv()
        spread_c(u, r)

    def forward(u, r):
        tf[u, r] = rcopy(u, slot(tg, u, 2, r), slot(tg, u, 2, r), ids(), dev(dy=1))
        cf[u, r] = rcopy(u, slot(cg, u, r, 2), slot(cg, u, r, 2), ids(), dev(dx=1))
        t_id, c_id = count[0] - 2, count[0] - 1
        tp[u, r].wait_recv()
        rcopy(u, slot(tg, u, 3, r, 0, 64), slot(tg, u, 2, r, 0, 64), t_id, dev(dy=1)).start()
        cp_[u, r].wait_recv()
        rcopy(u, slot(cg, u, r, 3, 0, 64), slot(cg, u, r, 2, 0, 64), c_id, dev(dx=1)).start()
        tm[u, r].wait_recv()
        rcopy(u, slot(tg, u, 1, r, 64, 64), slot(tg, u, 2, r, 64, 64), t_id, dev(dy=-1)).start()
        cm[u, r].wait_recv()
        rcopy(u, slot(cg, u, r, 1, 64, 64), slot(cg, u, r, 2, 64, 64), c_id, dev(dx=-1)).start()

    def tile(u, p, ry, hh):
        rows = pl.ds(pl.multiple_of(hh * 512 + u * 256, 256), 256)
        cols = pl.ds(pl.multiple_of(hh * 256, 256), 256)
        got = lax.dot_general(
            tg[u, ry, :, cols], cg[p, ry], (((0,), (0,)), ((), ())),
            preferred_element_type=jnp.float32,
        )
        part[rows, wide(p)] = got if ry == 0 else part[rows, wide(p)] + got

    def product(half, ry):
        cf[half, ry].wait_recv()
        for u, p in QUADS[:1] if half == 0 else QUADS[1:]:
            @pl.loop(0, 2)
            def _(hh):
                tile(u, p, ry, hh)

    def product_last(half):
        cf[half, 2].wait_recv()
        for r in range(4):
            tf[half, r].wait_recv()
        for u, p in QUADS[:1] if half == 0 else QUADS[1:]:
            for hh in (up, 1 - up):
                tile(u, p, 2, hh)
                for yy in (2 * u, 2 * u + 1):
                    core_copy(hh, yy, p).start()

    for u in range(2):
        G = GATHER[u]
        at(G[0], functools.partial(gather_first, u))
        for i, r in enumerate((3, 1, 2)):
            at(G[1 + i], functools.partial(gather_next, u, r))
        for i, r in enumerate((0, 3, 1, 2)):
            at(G[4 + i], functools.partial(forward, u, r))
        for i, r in enumerate((0, 3, 1)):
            at(G[8 + i], functools.partial(product, u, r))
        at(G[11], functools.partial(product_last, u))

    core_id = ids(8 * PIECES)

    def block(hh, yy, cc, lo=0, n=64):
        return pl.ds(pl.multiple_of(hh * 512 + yy * 128 + cc * 64 + lo, n), n)

    def wide(p):
        return pl.ds(p * WIDTH, WIDTH)

    def core_copy(hh, yy, p):
        return rcopy(
            CORE, part.at[block(hh, yy, 1 - c), wide(p)], core_in.at[hh, yy, :, wide(p)],
            core_id + (p * 2 + hh) * 4 + yy, dev(dc=1),
        )

    r = lax.rem(z - y + 8, 8)
    q = lax.rem(r, 4)
    end = q == 0
    up = jnp.where(r < 4, 1, 0)
    z_id = [ids(4 * SLICES), ids(4 * SLICES)]
    g_id = ids(SLICES)

    def chunk(hh, s, yy):
        return block(hh, yy, c, (s % PARTS) * SR, SR), wide(s // PARTS)

    def z_copy(way, hh, s, yy):
        return rcopy(
            CHAIN_Z, part.at[chunk(hh, s, yy)], z_in.at[way, s, yy],
            z_id[way] + s * 4 + yy, dev(dz=1 - 2 * way),
        )

    def g_copy(s, yy):
        return pltpu.make_async_remote_copy(
            src_ref=part.at[chunk(h, s, yy)], dst_ref=grad.at[s],
            send_sem=ssem.at[ROW], recv_sem=rsem.at[g_id + s],
            device_id=row_peer[yy], device_id_type=MESH,
        )

    def core_sum(hh, yy, p):
        core_copy(hh, yy, p).wait_recv()
        part[block(hh, yy, c), wide(p)] += core_in[hh, yy, :, wide(p)]

    def parts_of(j, way):
        u, p = QUADS[j]
        return [(p * PARTS + s, 2 * u + (i + 1 - way) % 2) for s in range(PARTS) for i in range(2)]

    def link(place, way, j, i):
        hh = up if way == 0 else 1 - up
        s, yy = parts_of(j, way)[i]
        if s % PARTS == 0:
            core_sum(hh, yy, s // PARTS)
        if i % 2 or place != (1 if way == 0 else 3):
            z_copy(way, hh, s, yy).wait_recv()
            rows, width = chunk(hh, s, yy)
            part[rows, width] += z_in[way, s, yy]
        z_copy(way, hh, s, yy).start()

    def far(j, i, way):
        s, yy = parts_of(j, way)[i]
        if s % PARTS == 0:
            core_sum(up, yy, s // PARTS)
        z_copy(way, up, s, yy).start()

    def last(s, yy):
        if s % PARTS == 0:
            core_sum(h, yy, s // PARTS)
        z_copy(0, h, s, yy).wait_recv()
        z_copy(1, h, s, yy).wait_recv()
        rows, width = chunk(h, s, yy)
        total = part[rows, width] + (z_in[0, s, yy] + z_in[1, s, yy])
        part[rows, width] = total

        @pl.when(yy == y)
        def _():
            grad[s] = total

        @pl.when(yy != y)
        def _():
            g_copy(s, yy).start()

    for j in range(4):
        for i in range(2 * PARTS):
            for way in range(2):
                for place in (1, 2, 3):
                    behind = place - 1 if way == 0 else 3 - place
                    at(CHAIN[j] + i * STEP + HOP * behind, functools.partial(link, place, way, j, i), place)
                if i % 2:
                    at(CHAIN[j] + i * STEP - STEP, functools.partial(far, j, i, way), 0)
            at(CHAIN[j] + i * STEP + 3 * HOP + 1, functools.partial(last, *parts_of(j, 1)[i]), 0)

    def adam(s):
        if s == 0:
            for f in fetch:
                f.wait()

        @pl.when(jnp.logical_not(end))
        def _():
            g_copy(s, 0).wait_recv()

        rows, width = pl.ds((s % PARTS) * SR, SR), wide(s // PARTS)
        g = grad[s]
        old = state[0, rows, width]
        m_new = first_beta * state[1, rows, width] + (1.0 - first_beta) * g
        s_new = second_beta * state[2, rows, width] + (1.0 - second_beta) * g * g
        update = m_new / first_fix / (jnp.sqrt(s_new / second_fix) + epsilon) + decay_rate * old
        new = old - learn_rate * update
        master_new[rows, width] = new
        moment_new[rows, width] = m_new
        second_new[rows, width] = s_new
        weights[x, h, y, c, rows, width] = new.astype(jnp.bfloat16)

    def da(d):
        return peer["a", d % 4]

    def db(d):
        return peer["b", d % 4]

    both = slice(None)
    side = dev(dc=1)
    side_id = ids()

    def spread(p):
        def unit(hh, a=0, b=0):
            xx, yy = place_of[a, b]
            return weights.at[xx, hh, yy, c, :, wide(p)]

        def pass_on(ref, to, sid=None):
            cp = rcopy(WEIGHTS, ref, ref, ids() if sid is None else sid, to)
            cp.start()
            return cp

        def to_side(hh, a=0, b=0):
            rcopy(SIDE, unit(hh, a, b), unit(hh, a, b), side_id, side).start()

        w_a, w_b, f_b, w_z, rest = {}, {}, {}, {}, {}

        def a_send(k):
            hh = (h, 1 - h)[k]
            for d in (1, -1, 2):
                w_a[k, d] = pass_on(unit(hh), da(d))

        def b_send(a, k, hh):
            if k == 0:
                rest[a] = ids()
            for d in (1, -1):
                w_b[a, k, d] = pass_on(unit(hh, a), db(d), None if d == (1, -1)[k] else rest[a])

        def first():
            for s in range(p * PARTS, (p + 1) * PARTS):
                adam(s)
            w_z[0] = pass_on(unit(h), dev(dz=4))
            a_send(0)
            b_send(0, 0, h)
            to_side(h)

        def second():
            w_z[0].wait_recv()
            a_send(1)
            b_send(0, 1, 1 - h)
            to_side(1 - h)

        def third(a, k):
            w_a[k, 2 if a == 2 else -a].wait_recv()
            b_send(a, k, (h, 1 - h)[k])
            if k == 1:
                to_side(both, a)

        def onward(a, k):
            d = (1, -1)[k]
            w_b[a, k, d].wait_recv()
            ref = unit((h, 1 - h)[k], a, -d)
            if k == 0:
                f_b[a] = ids()
            pass_on(ref, db(d), f_b[a])
            if k == 1:
                two = unit(both, a, 1)
                rcopy(WEIGHTS, two, two, rest[a], db(1)).wait_recv()
                to_side(both, a, 1)
                to_side(both, a, -1)

        def finish(a):
            two = unit(both, a, 2)
            rcopy(WEIGHTS, two, two, f_b[a], db(1)).wait_recv()
            to_side(both, a, 2)

        P_ = functools.partial
        T = TIMES
        out = [(T[0], first), (T[1], second)]
        for k in range(2):
            for i, a in enumerate((-1, 1, 2)):
                out.append((T[2 + k] + i * T[7], P_(third, a, k)))
            for i, a in enumerate((0, -1, 1, 2)):
                out.append((T[4 + k] + i * T[7], P_(onward, a, k)))
        for i, a in enumerate((0, -1, 1, 2)):
            out.append((T[6] + i * T[7], P_(finish, a)))
        return out

    for p in range(PIECES):
        ready = CHAIN[2 * p + 1] + 2 * PARTS * STEP + 3 * HOP + 1
        for when, stage in spread(p):
            at(ready + when, stage)

    events.sort(key=lambda e: e[:2])
    slots = sorted({int(e[0]) for e in events})
    for slot_ in slots:
        now = [e for e in events if int(e[0]) == slot_]
        for place in range(4):
            todo = [e[3] for e in now if e[2] == place]
            if todo:
                @pl.when(q == place)
                def _():
                    for what in todo:
                        what()
        for e in now:
            if e[2] is None:
                e[3]()

    all_side = rcopy(SIDE, weights.at[:, :, :, c], weights.at[:, :, :, 1 - c], side_id, side)
    all_side.wait_recv()
    all_side.wait_send()
    assert count[0] == N_SEM, count[0]
    for u in range(2):
        all_sent(u, 6 * 128 + 16 * 128 + 16 * 64)
    all_sent(CORE, 16 * 128)
    all_sent(WEIGHTS, 62 * 64)

    @pl.when(jnp.logical_not(end))
    def _():
        all_sent(CHAIN_Z, 32 * 64)

    @pl.when(end)
    def _():
        all_sent(CHAIN_Z, 16 * 64)
        all_sent(ROW, 12 * 64)


def copy_kernel(*refs):
    sem = refs[-1]
    copies = [pltpu.make_async_copy(refs[i], refs[4 + i], sem.at[i]) for i in (3, 0, 1, 2)]
    for cp in copies:
        cp.start()
    for cp in copies:
        cp.wait()


def write_out(*arrays):
    return pl.pallas_call(
        copy_kernel,
        out_shape=[jax.ShapeDtypeStruct(a.shape, a.dtype) for a in arrays],
        in_specs=[pl.BlockSpec(memory_space=pltpu.VMEM)] * 4,
        out_specs=[pl.BlockSpec(memory_space=pltpu.HBM)] * 4,
        scratch_shapes=[pltpu.SemaphoreType.DMA((4,))],
        compiler_params=pltpu.CompilerParams(vmem_limit_bytes=2**20),
    )(*arrays)


N_SEM = 195
VMEM_GRANT = 36 * 2**20


def on_device(tokens, cotangent, master, moment, second):
    vmem, hbm = pl.BlockSpec(memory_space=pltpu.VMEM), pl.BlockSpec(memory_space=pl.ANY)
    f32 = jax.ShapeDtypeStruct((64, 1024), jnp.float32)
    out = pl.pallas_call(
        kernel,
        out_shape=(f32, f32, f32, jax.ShapeDtypeStruct((4, 2, 4, 2, 64, 1024), jnp.bfloat16)),
        in_specs=[hbm] * 5,
        out_specs=(vmem, vmem, vmem, vmem),
        scratch_shapes=[
            pltpu.VMEM((2, 4, 512, 512), jnp.bfloat16),
            pltpu.VMEM((2, 4, 512, 512), jnp.bfloat16),
            pltpu.VMEM((1024, 1024), jnp.float32),
            pltpu.VMEM((2, 4, 64, 1024), jnp.float32),
            pltpu.VMEM((2, SLICES, 4, SR, WIDTH), jnp.float32),
            pltpu.VMEM((SLICES, SR, WIDTH), jnp.float32),
            pltpu.VMEM((3, 64, 1024), jnp.float32),
            pltpu.SemaphoreType.DMA((7,)),
            pltpu.SemaphoreType.DMA((N_SEM,)),
            pltpu.SemaphoreType.DMA((9,)),
        ],
        compiler_params=pltpu.CompilerParams(
            collective_id=0, has_side_effects=True, vmem_limit_bytes=VMEM_GRANT
        ),
    )(tokens, cotangent, master, moment, second)
    return write_out(*out[:3], out[3].reshape(4096, 1024))


def solution(mesh):
    placed = (
        P(("node", "local"), None),
        P(("node", "local"), None),
        P("node", "local"),
        P("node", "local"),
        P("node", "local"),
    )
    return jax.shard_map(
        on_device,
        mesh=mesh,
        in_specs=placed,
        out_specs=(P("node", "local"), P("node", "local"), P("node", "local"), P(None, "local")),
        check_vma=False,
    )
```

```python
import functools

import jax
import jax.numpy as jnp
from jax import lax
from jax.experimental import pallas as pl
from jax.experimental.pallas import tpu as pltpu
from jax.sharding import PartitionSpec as P

MESH = pl.DeviceIdType.MESH

first_beta = 0.9
second_beta = 0.95
learn_rate = 0.01
decay_rate = 0.1
epsilon = 1e-08
first_fix = 1.0 - 0.9**20
second_fix = 1.0 - 0.95**20

PIECES = 2
WIDTH = 1024 // PIECES
PARTS = 4
SR = 64 // PARTS
SLICES = PIECES * PARTS
QUADS = ((0, 0), (1, 0), (0, 1), (1, 1))
GATHER = (
    (0, 4, 5, 7, 9, 13, 16, 19, 20, 22, 23, 26),
    (14, 24, 25, 27, 31, 35, 38, 41, 42, 44, 45, 49),
)
CHAIN = (33, 52, 57.6, 63.2)
STEP, HOP = 0.7, 6.0
TIMES = (6.0, 14.0, 11.0, 20.0, 16.0, 25.0, 31.0, 1.0)


def kernel(
    tok, cot, master, moment, second,
    master_new, moment_new, second_new, weights,
    tg, cg, part, core_in, z_in, grad, state, ssem, rsem, lsem,
):
    fetch = [
        pltpu.make_async_copy(ref, state.at[i], lsem.at[6 + i])
        for i, ref in enumerate((master, moment, second))
    ]
    for f in fetch:
        f.start()
    node, l = lax.axis_index("node"), lax.axis_index("local")
    c = lax.rem(node, 2)
    y = lax.rem(lax.div(node, 2), 4)
    h = lax.rem(lax.div(node, 8), 2)
    x = lax.div(node, 16)
    z = h * 4 + l

    def around(v, n):
        return [v] + [lax.rem(v + d, n) for d in range(1, n)]

    xs, ys, zs = around(x, 4), around(y, 4), around(z, 8)

    def node_of(xx, hh, yy, cc):
        return ((xx * 2 + hh) * 4 + yy) * 2 + cc

    peer = {("x", d): (node_of(xs[d], h, y, c), l) for d in (1, 2, 3)}
    peer |= {("y", d): (node_of(x, h, ys[d], c), l) for d in (1, 2, 3)}
    peer |= {("z", d): (node_of(x, lax.div(zs[d], 4), y, c), lax.rem(zs[d], 4)) for d in (1, 7, 4)}
    peer["core", 1] = (node_of(x, h, y, 1 - c), l)
    for d in (1, 2, 3):
        for axis, one, two in (("a", "x", "y"), ("b", "y", "x")):
            peer[axis, d] = (jnp.where(c == 0, peer[one, d][0], peer[two, d][0]), l)
    row_peer = [(node_of(x, h, yy, c), l) for yy in range(4)]
    place_of = {
        (a, b): (jnp.where(c == 0, xs[a % 4], xs[b % 4]), jnp.where(c == 0, ys[b % 4], ys[a % 4]))
        for a in (0, -1, 1, 2) for b in (0, -1, 1, 2)
    }

    def dev(dx=0, dy=0, dz=0, dc=0):
        if dx:
            return peer["x", dx % 4]
        if dy:
            return peer["y", dy % 4]
        return peer["z", dz % 8] if dz else peer["core", dc]

    count = [0]

    def ids(n=1):
        first = count[0]
        count[0] += n
        return first

    CORE, CHAIN_Z, ROW, WEIGHTS, SIDE = range(2, 7)

    def rcopy(kind, src, dst, sid, to):
        return pltpu.make_async_remote_copy(
            src_ref=src, dst_ref=dst, send_sem=ssem.at[kind], recv_sem=rsem.at[sid],
            device_id=to, device_id_type=MESH,
        )

    def all_sent(kind, kib):
        rows = part.at[pl.ds(0, kib // 4)]
        rcopy(kind, rows, rows, 0, dev(dc=1)).wait_send()

    barrier = pltpu.get_barrier_semaphore()
    peers = [dev(dx=d) for d in (1, 2, 3)] + [dev(dy=d) for d in (1, 2, 3)]
    peers += [dev(dz=1), dev(dz=-1), dev(dz=4), dev(dc=1)]
    for p in peers:
        pl.semaphore_signal(barrier, inc=1, device_id=p, device_id_type=MESH)
    pl.semaphore_wait(barrier, len(peers))

    events = []

    def at(when, what, place=None):
        events.append((when, len(events), place, what))

    def slot(buf, u, ry, rx, lo=0, n=128):
        return buf.at[u, ry, pl.ds(rx * 128 + lo, n)]

    def t_cols(b, hh, u):
        return tok.at[:, pl.ds(pl.multiple_of(b * 1024 + hh * 512 + u * 256, 256), 256)]

    def c_cols(b, u):
        return cot.at[:, pl.ds(pl.multiple_of(b * 1024 + u * 512, 512), 512)]

    ta, ca, tp, tm, cp_, cm, tf, cf = ({} for _ in range(8))

    def spread_t(u, r):
        src = slot(tg, u, 0, r)
        tp[u, r] = rcopy(u, src, slot(tg, u, 3, r), ids(), dev(dy=1))
        tm[u, r] = rcopy(u, src, slot(tg, u, 1, r), ids(), dev(dy=-1))
        tp[u, r].start()
        tm[u, r].start()

    def spread_c(u, r):
        src = c_cols(y, u) if r == 0 else slot(cg, u, r, 0)
        cp_[u, r] = rcopy(u, src, slot(cg, u, r, 3), ids(), dev(dx=1))
        cm[u, r] = rcopy(u, src, slot(cg, u, r, 1), ids(), dev(dx=-1))
        cp_[u, r].start()
        cm[u, r].start()

    def gather_first(u):
        own = [
            pltpu.make_async_copy(
                t_cols(x, hh, u), tg.at[u, 0, pl.ds(0, 128), pl.ds(hh * 256, 256)], lsem.at[3 * u + hh]
            )
            for hh in range(2)
        ]
        own.append(pltpu.make_async_copy(c_cols(y, u), slot(cg, u, 0, 0), lsem.at[3 * u + 2]))
        for cp in own:
            cp.start()
        for d in (1, 3, 2):
            r = (4 - d) % 4
            ta[u, r] = rcopy(u, slot(tg, u, 0, r), slot(tg, u, 0, r), ids(), dev(dx=d))
            for hh in range(2):
                rcopy(u,
                    t_cols(xs[d], hh, u), tg.at[u, 0, pl.ds(r * 128, 128), pl.ds(hh * 256, 256)],
                    count[0] - 1, dev(dx=d),
                ).start()
            ca[u, r] = rcopy(u, c_cols(ys[d], u), slot(cg, u, r, 0), ids(), dev(dy=d))
            ca[u, r].start()
        spread_c(u, 0)
        for cp in own:
            cp.wait()
        spread_t(u, 0)

    def gather_next(u, r):
        ta[u, r].wait_recv()
        spread_t(u, r)
        ca[u, r].wait_recv()
        spread_c(u, r)

    def forward(u, r):
        tf[u, r] = rcopy(u, slot(tg, u, 2, r), slot(tg, u, 2, r), ids(), dev(dy=1))
        cf[u, r] = rcopy(u, slot(cg, u, r, 2), slot(cg, u, r, 2), ids(), dev(dx=1))
        t_id, c_id = count[0] - 2, count[0] - 1
        tp[u, r].wait_recv()
        rcopy(u, slot(tg, u, 3, r, 0, 64), slot(tg, u, 2, r, 0, 64), t_id, dev(dy=1)).start()
        cp_[u, r].wait_recv()
        rcopy(u, slot(cg, u, r, 3, 0, 64), slot(cg, u, r, 2, 0, 64), c_id, dev(dx=1)).start()
        tm[u, r].wait_recv()
        rcopy(u, slot(tg, u, 1, r, 64, 64), slot(tg, u, 2, r, 64, 64), t_id, dev(dy=-1)).start()
        cm[u, r].wait_recv()
        rcopy(u, slot(cg, u, r, 1, 64, 64), slot(cg, u, r, 2, 64, 64), c_id, dev(dx=-1)).start()

    def tile(u, p, ry, hh):
        rows = pl.ds(pl.multiple_of(hh * 512 + u * 256, 256), 256)
        cols = pl.ds(pl.multiple_of(hh * 256, 256), 256)
        got = lax.dot_general(
            tg[u, ry, :, cols], cg[p, ry], (((0,), (0,)), ((), ())),
            preferred_element_type=jnp.float32,
        )
        part[rows, wide(p)] = got if ry == 0 else part[rows, wide(p)] + got

    def product(half, ry):
        cf[half, ry].wait_recv()
        for u, p in QUADS[:1] if half == 0 else QUADS[1:]:
            @pl.loop(0, 2)
            def _(hh):
                tile(u, p, ry, hh)

    def product_last(half):
        cf[half, 2].wait_recv()
        for r in range(4):
            tf[half, r].wait_recv()
        for u, p in QUADS[:1] if half == 0 else QUADS[1:]:
            for hh in (up, 1 - up):
                tile(u, p, 2, hh)
                for yy in (2 * u, 2 * u + 1):
                    core_copy(hh, yy, p).start()

    for u in range(2):
        G = GATHER[u]
        at(G[0], functools.partial(gather_first, u))
        for i, r in enumerate((3, 1, 2)):
            at(G[1 + i], functools.partial(gather_next, u, r))
        for i, r in enumerate((0, 3, 1, 2)):
            at(G[4 + i], functools.partial(forward, u, r))
        for i, r in enumerate((0, 3, 1)):
            at(G[8 + i], functools.partial(product, u, r))
        at(G[11], functools.partial(product_last, u))

    core_id = ids(8 * PIECES)

    def block(hh, yy, cc, lo=0, n=64):
        return pl.ds(pl.multiple_of(hh * 512 + yy * 128 + cc * 64 + lo, n), n)

    def wide(p):
        return pl.ds(p * WIDTH, WIDTH)

    def core_copy(hh, yy, p):
        return rcopy(
            CORE, part.at[block(hh, yy, 1 - c), wide(p)], core_in.at[hh, yy, :, wide(p)],
            core_id + (p * 2 + hh) * 4 + yy, dev(dc=1),
        )

    r = lax.rem(z - y + 8, 8)
    q = lax.rem(r, 4)
    end = q == 0
    up = jnp.where(r < 4, 1, 0)
    z_id = [ids(4 * SLICES), ids(4 * SLICES)]
    g_id = ids(SLICES)

    def chunk(hh, s, yy):
        return block(hh, yy, c, (s % PARTS) * SR, SR), wide(s // PARTS)

    def z_copy(way, hh, s, yy):
        return rcopy(
            CHAIN_Z, part.at[chunk(hh, s, yy)], z_in.at[way, s, yy],
            z_id[way] + s * 4 + yy, dev(dz=1 - 2 * way),
        )

    def g_copy(s, yy):
        return pltpu.make_async_remote_copy(
            src_ref=part.at[chunk(h, s, yy)], dst_ref=grad.at[s],
            send_sem=ssem.at[ROW], recv_sem=rsem.at[g_id + s],
            device_id=row_peer[yy], device_id_type=MESH,
        )

    def core_sum(hh, yy, p):
        core_copy(hh, yy, p).wait_recv()
        part[block(hh, yy, c), wide(p)] += core_in[hh, yy, :, wide(p)]

    def parts_of(j, way):
        u, p = QUADS[j]
        return [(p * PARTS + s, 2 * u + (i + 1 - way) % 2) for s in range(PARTS) for i in range(2)]

    def link(place, way, j, i):
        hh = up if way == 0 else 1 - up
        s, yy = parts_of(j, way)[i]
        if s % PARTS == 0:
            core_sum(hh, yy, s // PARTS)
        if i % 2 or place != (1 if way == 0 else 3):
            z_copy(way, hh, s, yy).wait_recv()
            rows, width = chunk(hh, s, yy)
            part[rows, width] += z_in[way, s, yy]
        z_copy(way, hh, s, yy).start()

    def far(j, i, way):
        s, yy = parts_of(j, way)[i]
        if s % PARTS == 0:
            core_sum(up, yy, s // PARTS)
        z_copy(way, up, s, yy).start()

    def last(s, yy):
        if s % PARTS == 0:
            core_sum(h, yy, s // PARTS)
        z_copy(0, h, s, yy).wait_recv()
        z_copy(1, h, s, yy).wait_recv()
        rows, width = chunk(h, s, yy)
        total = part[rows, width] + (z_in[0, s, yy] + z_in[1, s, yy])
        part[rows, width] = total

        @pl.when(yy == y)
        def _():
            grad[s] = total

        @pl.when(yy != y)
        def _():
            g_copy(s, yy).start()

    for j in range(4):
        for i in range(2 * PARTS):
            for way in range(2):
                for place in (1, 2, 3):
                    behind = place - 1 if way == 0 else 3 - place
                    at(CHAIN[j] + i * STEP + HOP * behind, functools.partial(link, place, way, j, i), place)
                if i % 2:
                    at(CHAIN[j] + i * STEP - STEP, functools.partial(far, j, i, way), 0)
            at(CHAIN[j] + i * STEP + 3 * HOP + 1, functools.partial(last, *parts_of(j, 1)[i]), 0)

    def adam(s):
        if s == 0:
            for f in fetch:
                f.wait()

        @pl.when(jnp.logical_not(end))
        def _():
            g_copy(s, 0).wait_recv()

        rows, width = pl.ds((s % PARTS) * SR, SR), wide(s // PARTS)
        g = grad[s]
        old = state[0, rows, width]
        m_new = first_beta * state[1, rows, width] + (1.0 - first_beta) * g
        s_new = second_beta * state[2, rows, width] + (1.0 - second_beta) * g * g
        update = m_new / first_fix / (jnp.sqrt(s_new / second_fix) + epsilon) + decay_rate * old
        new = old - learn_rate * update
        master_new[rows, width] = new
        moment_new[rows, width] = m_new
        second_new[rows, width] = s_new
        weights[x, h, y, c, rows, width] = new.astype(jnp.bfloat16)

    def da(d):
        return peer["a", d % 4]

    def db(d):
        return peer["b", d % 4]

    both = slice(None)
    side = dev(dc=1)
    side_id = ids()

    def spread(p):
        def unit(hh, a=0, b=0):
            xx, yy = place_of[a, b]
            return weights.at[xx, hh, yy, c, :, wide(p)]

        def pass_on(ref, to, sid=None):
            cp = rcopy(WEIGHTS, ref, ref, ids() if sid is None else sid, to)
            cp.start()
            return cp

        def to_side(hh, a=0, b=0):
            rcopy(SIDE, unit(hh, a, b), unit(hh, a, b), side_id, side).start()

        w_a, w_b, f_b, w_z, rest = {}, {}, {}, {}, {}

        def a_send(k):
            hh = (h, 1 - h)[k]
            for d in (1, -1, 2):
                w_a[k, d] = pass_on(unit(hh), da(d))

        def b_send(a, k, hh):
            if k == 0:
                rest[a] = ids()
            for d in (1, -1):
                w_b[a, k, d] = pass_on(unit(hh, a), db(d), None if d == (1, -1)[k] else rest[a])

        def first():
            for s in range(p * PARTS, (p + 1) * PARTS):
                adam(s)
            w_z[0] = pass_on(unit(h), dev(dz=4))
            a_send(0)
            b_send(0, 0, h)
            to_side(h)

        def second():
            w_z[0].wait_recv()
            a_send(1)
            b_send(0, 1, 1 - h)
            to_side(1 - h)

        def third(a, k):
            w_a[k, 2 if a == 2 else -a].wait_recv()
            b_send(a, k, (h, 1 - h)[k])
            if k == 1:
                to_side(both, a)

        def onward(a, k):
            d = (1, -1)[k]
            w_b[a, k, d].wait_recv()
            ref = unit((h, 1 - h)[k], a, -d)
            if k == 0:
                f_b[a] = ids()
            pass_on(ref, db(d), f_b[a])
            if k == 1:
                two = unit(both, a, 1)
                rcopy(WEIGHTS, two, two, rest[a], db(1)).wait_recv()
                to_side(both, a, 1)
                to_side(both, a, -1)

        def finish(a):
            two = unit(both, a, 2)
            rcopy(WEIGHTS, two, two, f_b[a], db(1)).wait_recv()
            to_side(both, a, 2)

        P_ = functools.partial
        T = TIMES
        out = [(T[0], first), (T[1], second)]
        for k in range(2):
            for i, a in enumerate((-1, 1, 2)):
                out.append((T[2 + k] + i * T[7], P_(third, a, k)))
            for i, a in enumerate((0, -1, 1, 2)):
                out.append((T[4 + k] + i * T[7], P_(onward, a, k)))
        for i, a in enumerate((0, -1, 1, 2)):
            out.append((T[6] + i * T[7], P_(finish, a)))
        return out

    for p in range(PIECES):
        ready = CHAIN[2 * p + 1] + 2 * PARTS * STEP + 3 * HOP + 1
        for when, stage in spread(p):
            at(ready + when, stage)

    events.sort(key=lambda e: e[:2])
    slots = sorted({int(e[0]) for e in events})
    for slot_ in slots:
        now = [e for e in events if int(e[0]) == slot_]
        for place in range(4):
            todo = [e[3] for e in now if e[2] == place]
            if todo:
                @pl.when(q == place)
                def _():
                    for what in todo:
                        what()
        for e in now:
            if e[2] is None:
                e[3]()

    all_side = rcopy(SIDE, weights.at[:, :, :, c], weights.at[:, :, :, 1 - c], side_id, side)
    all_side.wait_recv()
    all_side.wait_send()
    assert count[0] == N_SEM, count[0]
    for u in range(2):
        all_sent(u, 6 * 128 + 16 * 128 + 16 * 64)
    all_sent(CORE, 16 * 128)
    all_sent(WEIGHTS, 62 * 64)

    @pl.when(jnp.logical_not(end))
    def _():
        all_sent(CHAIN_Z, 32 * 64)

    @pl.when(end)
    def _():
        all_sent(CHAIN_Z, 16 * 64)
        all_sent(ROW, 12 * 64)


def copy_kernel(*refs):
    sem = refs[-1]
    copies = [pltpu.make_async_copy(refs[i], refs[4 + i], sem.at[i]) for i in (3, 0, 1, 2)]
    for cp in copies:
        cp.start()
    for cp in copies:
        cp.wait()


def write_out(*arrays):
    return pl.pallas_call(
        copy_kernel,
        out_shape=[jax.ShapeDtypeStruct(a.shape, a.dtype) for a in arrays],
        in_specs=[pl.BlockSpec(memory_space=pltpu.VMEM)] * 4,
        out_specs=[pl.BlockSpec(memory_space=pltpu.HBM)] * 4,
        scratch_shapes=[pltpu.SemaphoreType.DMA((4,))],
        compiler_params=pltpu.CompilerParams(vmem_limit_bytes=2**20),
    )(*arrays)


N_SEM = 195
VMEM_GRANT = 36 * 2**20


def on_device(tokens, cotangent, master, moment, second):
    vmem, hbm = pl.BlockSpec(memory_space=pltpu.VMEM), pl.BlockSpec(memory_space=pl.ANY)
    f32 = jax.ShapeDtypeStruct((64, 1024), jnp.float32)
    out = pl.pallas_call(
        kernel,
        out_shape=(f32, f32, f32, jax.ShapeDtypeStruct((4, 2, 4, 2, 64, 1024), jnp.bfloat16)),
        in_specs=[hbm] * 5,
        out_specs=(vmem, vmem, vmem, vmem),
        scratch_shapes=[
            pltpu.VMEM((2, 4, 512, 512), jnp.bfloat16),
            pltpu.VMEM((2, 4, 512, 512), jnp.bfloat16),
            pltpu.VMEM((1024, 1024), jnp.float32),
            pltpu.VMEM((2, 4, 64, 1024), jnp.float32),
            pltpu.VMEM((2, SLICES, 4, SR, WIDTH), jnp.float32),
            pltpu.VMEM((SLICES, SR, WIDTH), jnp.float32),
            pltpu.VMEM((3, 64, 1024), jnp.float32),
            pltpu.SemaphoreType.DMA((7,)),
            pltpu.SemaphoreType.DMA((N_SEM,)),
            pltpu.SemaphoreType.DMA((9,)),
        ],
        compiler_params=pltpu.CompilerParams(
            collective_id=0, has_side_effects=True, vmem_limit_bytes=VMEM_GRANT
        ),
    )(tokens, cotangent, master, moment, second)
    return write_out(*out[:3], out[3].reshape(4096, 1024))


def solution(mesh):
    placed = (
        P(("node", "local"), None),
        P(("node", "local"), None),
        P("node", "local"),
        P("node", "local"),
        P("node", "local"),
    )
    return jax.shard_map(
        on_device,
        mesh=mesh,
        in_specs=placed,
        out_specs=(P("node", "local"), P("node", "local"), P("node", "local"), P(None, "local")),
        check_vma=False,
    )
```
